256 devices in a mesh: gx: 32 (over y, x, core), gy: 8 (over z).
Axes of the slice: x: 4, y: 4, z: 8, core: 2. Of those that a mesh axis runs over, the one named last changes fastest.
Arguments:
- displacement: float32 [3, 256, 128, 128], P(None, 'gx', 'gy'), may hold values from -6 to 6
- load_vector: float32 [3, 256, 128, 128], P(None, 'gx', 'gy'), may hold values from -6 to 6
- diag_inverse: float32 [3, 3, 256, 128, 128], P(None, None, 'gx', 'gy'), may hold values from -0.75 to 2.5, as said below
- stiffness: float32 [256, 128, 128], P('gx', 'gy'), may hold values from 0.3 to 3
- stencil: float32 [13, 3, 3], replicated, may hold values from -0.4 to 0.4
- colour: int32 [256, 128, 128], P('gx', 'gy'), may hold values from 0 to 7, as said below
Outputs:
- relaxed: float32 [3, 256, 128, 128], P(None, 'gx', 'gy')
The draws below stay inside these ranges and needn't reach their ends.
Inputs may be any that keep to these rules, and one draw needn't show every extreme that they name: colour at node (i, j, k) depends only on (i mod 2, j mod 2, k mod 2), and the eight parity classes carry the eight different colours. Each node's 3x3 block of diag_inverse is symmetric positive definite.
All inputs are finite; a program needn't handle non-finite values.
Results may differ from the reference program's by a relative error of at most 0.00002.
Values sent between devices are 32-bit elements; how exact they have to be, the bound alone decides.
No kernel may reach another device: no remote copies, remote signals or barrier semaphores. Data moves between devices by JAX's collectives and lax.ppermute only.
A program may use at most 128 MiB of HBM per device.

```python
import math
import jax
import jax.numpy as jnp

NZ = 128
NX = 256
NY = 128


def draw_colour(key, part):
    key = jax.random.fold_in(key, 11)
    labels = jax.random.permutation(key, 8).astype(jnp.int32)
    parity_x = jnp.arange(NX, dtype=jnp.int32) % 2
    parity_y = jnp.arange(NY, dtype=jnp.int32) % 2
    parity_z = jnp.arange(NZ, dtype=jnp.int32) % 2
    classes = 4 * parity_x[:, None, None] + 2 * parity_y[None, :, None] + parity_z[None, None, :]
    return jnp.take(labels, classes)


def draw_diag_inverse(key, part):
    key = jax.random.fold_in(key, 5)
    key_diag, key_off = jax.random.split(key)
    logs = jax.random.uniform(key_diag, (3, NX, NY, NZ), jnp.float32, jnp.log(0.4), jnp.log(1.6))
    scales = jnp.exp(logs)
    roots = jnp.sqrt(scales)
    offs = jax.random.uniform(key_off, (3, NX, NY, NZ), jnp.float32, -1.0, 1.0)
    entry_01 = 0.3 * offs[0] * roots[0] * roots[1]
    entry_02 = 0.3 * offs[1] * roots[0] * roots[2]
    entry_12 = 0.3 * offs[2] * roots[1] * roots[2]
    row_zero = jnp.stack([scales[0], entry_01, entry_02])
    row_one = jnp.stack([entry_01, scales[1], entry_12])
    row_two = jnp.stack([entry_02, entry_12, scales[2]])
    return jnp.stack([row_zero, row_one, row_two]).astype(jnp.float32)


def level_of(key, shape, cuts, low, top_value):
    level, own = 1.0, jax.random.fold_in(key, 6)
    for position, blocks in cuts:
        heights = jnp.exp(jax.random.uniform(jax.random.fold_in(own, position), (blocks,), jnp.float32, low / len(cuts), top_value / len(cuts)))
        level = level * jnp.repeat(heights, shape[position] // blocks).reshape([-1 if axis == position else 1 for axis in range(len(shape))])
    return level


def normal_values(stream_key, dims, deviation, most, shards=(), held_as=jnp.bfloat16):
    entries = jax.random.normal(stream_key, dims, jnp.float32) * deviation
    if len(shards) > 0:
        entries = level_of(stream_key, dims, shards, -0.22, 0.18) * entries
    return jnp.clip(entries, min=-most, max=most).astype(held_as)


def setup_inputs(seed: int = 0) -> dict:
    splits = jax.random.split(jax.random.key(seed), 7)
    return {
        "displacement": normal_values(splits[0], (3, NX, NY, NZ), 1.0, 6.0, ((1, 32), (2, 8)), jnp.float32),
        "load_vector": normal_values(splits[1], (3, NX, NY, NZ), 1.0, 6.0, ((1, 32), (2, 8)), jnp.float32),
        "diag_inverse": draw_diag_inverse(jax.random.fold_in(splits[6], 71), 0),
        "stiffness": jnp.clip(jnp.exp(math.log(3.0) - 2.3025851 * jax.random.uniform(splits[3], (NX, NY, NZ), jnp.float32) ** level_of(splits[3], (NX, NY, NZ), ((0, 32), (1, 8)), -0.2, 0.2)), 0.3, 3.0),
        "stencil": normal_values(splits[4], (13, 3, 3), 0.08, 0.4, (), jnp.float32),
        "colour": draw_colour(jax.random.fold_in(splits[6], 71), 0),
    }


forward_offsets = [(first, second, third) for first in (-1, 0, 1) for second in (-1, 0, 1) for third in (-1, 0, 1) if (first, second, third) > (0, 0, 0)]


def node_product(matrix, field):
    return matrix[:, 0] * field[0] + matrix[:, 1] * field[1] + matrix[:, 2] * field[2]


def couple(field_pad, stiff_pad, stencil, start_x, start_y, size_x, size_y, size_z):
    centre = stiff_pad[start_x:start_x + size_x, start_y:start_y + size_y, 1:1 + size_z]
    summed = jnp.zeros((3, size_x, size_y, size_z), jnp.float32)
    for number, offset in enumerate(forward_offsets):
        for orient in (1, -1):
            coupling_block = stencil[number] if orient == 1 else stencil[number].T
            step_x = orient * offset[0]
            step_y = orient * offset[1]
            step_z = orient * offset[2]
            low_x = start_x + step_x
            low_y = start_y + step_y
            low_z = 1 + step_z
            neighbour = field_pad[:, low_x:low_x + size_x, low_y:low_y + size_y, low_z:low_z + size_z]
            weight = 0.5 * (centre + stiff_pad[low_x:low_x + size_x, low_y:low_y + size_y, low_z:low_z + size_z])
            summed = summed + weight * node_product(coupling_block[:, :, None, None, None], neighbour)
    return summed


def reference(displacement, load_vector, diag_inverse, stiffness, stencil, colour):
    stiff_pad = jnp.pad(stiffness, 1)
    field = displacement
    for colour_now in range(8):
        field_pad = jnp.pad(field, ((0, 0), (1, 1), (1, 1), (1, 1)))
        coupled = couple(field_pad, stiff_pad, stencil, 1, 1, NX, NY, NZ)
        update = node_product(diag_inverse, load_vector - coupled)
        field = jnp.where(colour[None] == colour_now, update, field)
    return field
```

```python
import jax
import jax.numpy as jnp
from jax import lax
from jax.experimental import pallas as pl
from jax.experimental.pallas import tpu as pltpu
from jax.sharding import PartitionSpec as P

XD, YD, ZD = 8, 16, 128
L = 6
PAD = 8
INV = (0, 1, 2, 4, 5, 8)
F32 = jnp.float32

offsets = [
    (a, b, c)
    for a in (-1, 0, 1)
    for b in (-1, 0, 1)
    for c in (-1, 0, 1)
    if (a, b, c) > (0, 0, 0)
]

NF = 16 * 8
NS = 18 * 8
XF = 4 * L * 4 * 4
XS = 18 * L * 4


def lanes(rows):
    return lax.broadcasted_iota(jnp.int32, (rows, 128), 1)


def low(rows):
    return lanes(rows) < 64


def gather(v, idx):
    return jnp.take_along_axis(v, idx, axis=1, mode="promise_in_bounds")


def split_idx(rows, first):
    lane = lanes(rows)
    return jnp.where(lane < 64, 2 * lane + first, 2 * lane - 127 - first)


def swap(v):
    return pltpu.roll(v, 64, 1)


def parity(cls):
    return lax.shift_right_logical(cls, 2), lax.shift_right_logical(cls, 1) & 1, cls & 1


def load_rows(nat, first, cls_row, y1, count):
    return nat[pl.ds(first + cls_row + 2 * y1, count, stride=32), :]


def static_slices(load_ref, inv_ref):
    return [(load_ref, i * 128) for i in range(3)] + [(inv_ref, i * 128) for i in INV]


def field_slices(disp_ref, stiff_ref):
    return [(disp_ref, 0), (disp_ref, 128), (disp_ref, 256), (stiff_ref, 0)]


def pack_y_kernel(order_ref, disp_ref, load_ref, inv_ref, stiff_ref, lo_ref, hi_ref, near_s, far_s):
    lowm = low(8)
    idx_e = split_idx(8, 0)
    for comp, (ref, first) in enumerate(field_slices(disp_ref, stiff_ref)):
        for py in range(2):
            for out, y1 in ((lo_ref, 0), (hi_ref, 6)):
                a = ref[pl.ds(first + py + 2 * y1, 8, stride=16), :]
                b = ref[pl.ds(first + py + 2 * y1 + 2, 8, stride=16), :]
                if comp == 3:
                    a, b = 0.5 * a, 0.5 * b
                a, b = gather(a, idx_e), gather(b, idx_e)
                row = (comp * 4 + py * 2) * 8
                out[pl.ds(row, 8), :] = jnp.where(lowm, a, swap(b))
                out[pl.ds(row + 8, 8), :] = jnp.where(lowm, swap(a), b)
    for r in range(2):
        px, py, pz = zip(*[parity(order_ref[4 * r + k]) for k in range(3)])
        cls_row = [px[k] * 16 + py[k] for k in range(3)]
        for side, out in ((0, lo_ref), (1, hi_ref)):
            near, far = (0, 1) if side == 0 else (7, 6)
            idx_near = [split_idx(4, pz[k] if side == 0 else 1 - pz[k]) for k in range(3)]
            idx_far = [split_idx(4, 1 - pz[k] if side == 0 else pz[k]) for k in range(3)]
            for a, (ref, first) in enumerate(static_slices(load_ref, inv_ref)):
                v = [load_rows(ref, first, cls_row[k], near, 4) for k in range(3)]
                n0 = gather(v[0], idx_near[0])
                f0 = gather(load_rows(ref, first, cls_row[0], far, 4), idx_far[0])
                near_s[0:2, :] = n0[0:2]
                near_s[4:6, :] = n0[2:4]
                far_s[0:2, :] = f0[0:2]
                far_s[4:6, :] = f0[2:4]
                for k in (1, 2):
                    n = gather(v[k], idx_near[k])
                    f = gather(v[k], idx_far[k])
                    near_s[1 + k : 2 + k, :] = n[0:1]
                    near_s[5 + k : 6 + k, :] = n[3:4]
                    far_s[1 + k : 2 + k, :] = f[1:2]
                    far_s[5 + k : 6 + k, :] = f[2:3]
                nv, fv = near_s[...], far_s[...]
                out[pl.ds(NF + (r * 9 + a) * 8, 8), :] = (
                    jnp.where(lowm, nv, fv) if side == 0 else jnp.where(lowm, fv, nv)
                )


def convert_kernel(order_ref, disp_ref, load_ref, inv_ref, stiff_ref, f_ref, s_ref, own0_ref, own1_ref):
    lowm = low(8)
    low4 = low(4)
    idx_e = split_idx(8, 0)
    zero = jnp.zeros((8, 128), F32)
    for comp, (ref, first) in enumerate(field_slices(disp_ref, stiff_ref)):
        for py in range(2):
            ev, od = [], []
            for y1 in range(8):
                v = ref[pl.ds(first + py + 2 * y1, 8, stride=16), :]
                if comp == 3:
                    v = 0.5 * v
                v = gather(v, idx_e)
                ev.append(v)
                od.append(swap(v))
            for l in range(L):
                e0, o0 = (ev[l - 2], od[l - 2]) if l >= 2 else (zero, zero)
                e1, o1 = (ev[l + 4], od[l + 4]) if l <= 3 else (zero, zero)
                row = ((comp * L + l) * 4 + py * 2) * 8
                f_ref[pl.ds(row, 8), :] = jnp.where(lowm, e0, o1)
                f_ref[pl.ds(row + 8, 8), :] = jnp.where(lowm, o0, e1)
    zero4 = jnp.zeros((4, 128), F32)
    for r, own in ((0, own0_ref), (1, own1_ref)):
        for k in range(4):
            px, py, pz = parity(order_ref[4 * r + k])
            cls_row = px * 16 + py
            idx0, idx1 = split_idx(4, pz), split_idx(4, 1 - pz)
            for a, (ref, first) in enumerate(static_slices(load_ref, inv_ref)):
                rows = [load_rows(ref, first, cls_row, y1, 4) for y1 in range(8)]
                for l in range(L):
                    v0 = gather(rows[l - 2], idx0) if l >= 2 else zero4
                    v1 = gather(rows[l + 4], idx1) if l <= 3 else zero4
                    v = jnp.where(low4, v0, v1)
                    srow = ((r * 9 + a) * L + l) * 8
                    if k == 0:
                        s_ref[pl.ds(srow, 2), :] = v[0:2]
                        s_ref[pl.ds(srow + 4, 2), :] = v[2:4]
                    else:
                        own[pl.ds((((k - 1) * 9 + a) * L + l) * 4, 4), :] = v
                        if k < 3:
                            s_ref[pl.ds(srow + 1 + k, 1), :] = v[0:1]
                            s_ref[pl.ds(srow + 5 + k, 1), :] = v[3:4]


def add_y(v, l, below, above, lowm):
    if l == 0:
        return jnp.where(lowm, below, v)
    if l == 1:
        return jnp.where(lowm, swap(below), v)
    if l == 4:
        return jnp.where(lowm, v, swap(above))
    if l == 5:
        return jnp.where(lowm, v, above)
    return v


def put_pair(xl_ref, xr_ref, row, v, w):
    sub = lax.broadcasted_iota(jnp.int32, (8, 128), 0) < 4
    xl_ref[pl.ds(row, 8), :] = jnp.where(sub, v, pltpu.roll(w, 4, 0))
    xr_ref[pl.ds(row, 8), :] = jnp.where(sub, pltpu.roll(v, 4, 0), w)


def y_masks():
    gy = lax.axis_index("gy")
    return (
        jnp.where(gy > 0, 1.0, 0.0).astype(F32),
        jnp.where(gy < lax.axis_size("gy") - 1, 1.0, 0.0).astype(F32),
    )


def x_masks():
    gx = lax.axis_index("gx")
    return (
        jnp.where(gx > 0, 1.0, 0.0).astype(F32),
        jnp.where(gx < lax.axis_size("gx") - 1, 1.0, 0.0).astype(F32),
    )


def pack_x_fields(comps, f_ref, below_ref, above_ref, xl_ref, xr_ref):
    lowm = low(8)
    m_below, m_above = y_masks()
    for comp in range(comps):
        for half in range(2):
            below = [below_ref[pl.ds((comp * 4 + 2 * half + i) * 8, 8), :] * m_below for i in range(2)]
            above = [above_ref[pl.ds((comp * 4 + 2 * half + i) * 8, 8), :] * m_above for i in range(2)]
            for l in range(L):
                row = (comp * L + l) * 4 + 2 * half
                v = [add_y(f_ref[pl.ds((row + i) * 8, 8), :], l, below[i], above[i], lowm) for i in range(2)]
                put_pair(xl_ref, xr_ref, row * 4, v[0], v[1])


def pack_x_kernel(f_ref, s_ref, below_ref, above_ref, xl_ref, xr_ref):
    pack_x_fields(4, f_ref, below_ref, above_ref, xl_ref, xr_ref)
    lowm = low(8)
    m_below, m_above = y_masks()
    for ra in range(18):
        below = below_ref[pl.ds(NF + ra * 8, 8), :] * m_below
        above = above_ref[pl.ds(NF + ra * 8, 8), :] * m_above
        for l in range(0, L, 2):
            row = ra * L + l
            v = [add_y(s_ref[pl.ds((row + i) * 8, 8), :], l + i, below, above, lowm) for i in range(2)]
            put_pair(xl_ref, xr_ref, XF + row * 4, v[0], v[1])


def pack_x2_kernel(f_ref, below_ref, above_ref, xl_ref, xr_ref):
    pack_x_fields(3, f_ref, below_ref, above_ref, xl_ref, xr_ref)


def v_row(cls, shifted, comp, ext):
    return PAD + (((cls * 2 + shifted) * 4 + comp) * 8 + ext) * 8


def fill_class(v_ref, cls, pz, comp):
    lane = lanes(8)
    shift = jnp.where(pz == 1, 1, 127) if not isinstance(pz, int) else (1 if pz == 1 else 127)
    edge = jnp.where(pz == 1, 0, 63) if not isinstance(pz, int) else (0 if pz == 1 else 63)
    keep = (lane & 63) != edge
    base = v_row(cls, 0, comp, 0)
    moved = v_row(cls, 1, comp, 0)
    for l in range(L):
        v = v_ref[pl.ds(base + (l + 1) * 8, 8), :]
        w = jnp.where(keep, pltpu.roll(v, shift, 1), 0.0)
        v_ref[pl.ds(moved + (l + 1) * 8, 8), :] = w
        if l == 0:
            v_ref[pl.ds(base + 56, 8), :] = swap(v)
            v_ref[pl.ds(moved + 56, 8), :] = swap(w)
        if l == L - 1:
            v_ref[pl.ds(base, 8), :] = swap(v)
            v_ref[pl.ds(moved, 8), :] = swap(w)


def fill_fields(comps, v_ref, e_ref, rl_ref, xl_ref, xr_ref, rr_ref):
    m_left, m_right = x_masks()
    for comp in range(comps):
        for l in range(L):
            for p in range(4):
                row = ((comp * L + l) * 4 + p) * 4
                at = (l * 4 + p) * 16
                e_ref[pl.ds(at, 4), :] = rl_ref[pl.ds(row, 4), :] * m_left
                e_ref[pl.ds(at + 4, 4), :] = xl_ref[pl.ds(row, 4), :]
                e_ref[pl.ds(at + 8, 4), :] = xr_ref[pl.ds(row, 4), :]
                e_ref[pl.ds(at + 12, 4), :] = rr_ref[pl.ds(row, 4), :] * m_right
        for l in range(L):
            for p in range(4):
                for px in range(2):
                    v_ref[pl.ds(v_row(px * 4 + p, 0, comp, l + 1), 8), :] = e_ref[
                        pl.ds((l * 4 + p) * 16 + px, 8, stride=2), :
                    ]
        for cls in range(8):
            fill_class(v_ref, cls, cls & 1, comp)


def fill_statics(r, st_ref, rl_ref, xl_ref, xr_ref, rr_ref, own_ref, below_ref, above_ref):
    m_left, m_right = x_masks()
    m_below, m_above = y_masks()
    lowm = low(1)
    zero = jnp.zeros((8, 128), F32)
    for a in range(9):
        below = below_ref[pl.ds(NF + (r * 9 + a) * 8, 8), :] * m_below
        above = above_ref[pl.ds(NF + (r * 9 + a) * 8, 8), :] * m_above
        for l in range(L):
            srow = XF + ((r * 9 + a) * L + l) * 4
            left, right = rl_ref[pl.ds(srow, 4), :] * m_left, rr_ref[pl.ds(srow, 4), :] * m_right
            own_l, own_r = xl_ref[pl.ds(srow, 4), :], xr_ref[pl.ds(srow, 4), :]
            at = (a * L + l) * 8
            st_ref[pl.ds(at, 2), :] = left[0:2]
            st_ref[pl.ds(at + 2, 2), :] = own_l[0:2]
            st_ref[pl.ds(at + 4, 2), :] = own_r[0:2]
            st_ref[pl.ds(at + 6, 2), :] = right[0:2]
            for k in (1, 2, 3):
                at = ((k * 9 + a) * L + l) * 8
                st_ref[pl.ds(at, 8), :] = zero
                st_ref[pl.ds(at + 2, 4), :] = own_ref[pl.ds((((k - 1) * 9 + a) * L + l) * 4, 4), :]
                if k < 3:
                    st_ref[pl.ds(at + 1, 1), :] = left[1 + k : 2 + k]
                    st_ref[pl.ds(at + 2, 1), :] = own_l[1 + k : 2 + k]
                    st_ref[pl.ds(at + 5, 1), :] = own_r[1 + k : 2 + k]
                    st_ref[pl.ds(at + 6, 1), :] = right[1 + k : 2 + k]
                    for q in range(2):
                        at_q = at + 3 + q
                        if l == 1:
                            st_ref[pl.ds(at_q, 1), :] = jnp.where(
                                lowm, below[1 + k + 4 * q : 2 + k + 4 * q], st_ref[pl.ds(at_q, 1), :]
                            )
                        if l == 4:
                            st_ref[pl.ds(at_q, 1), :] = jnp.where(
                                lowm, st_ref[pl.ds(at_q, 1), :], above[1 + k + 4 * q : 2 + k + 4 * q]
                            )


def relax(cls, k, v_ref, st_ref, stencil_ref):
    px, py, pz = parity(cls)
    by_x = {0: 0, -1: px - 1, 1: px}
    by_y = {0: 0, -1: (py - 1) * 8, 1: py * 8}
    by_z = {0: 0, -1: 1 - pz, 1: pz}
    centre = [v_ref[pl.ds(v_row(cls, 0, 3, l + 1), 8), :] for l in range(L)]
    acc = [[None] * L for _ in range(3)]
    for number, (a, b, c) in enumerate(offsets):
        for orient in (1, -1):
            da, db, dc = orient * a, orient * b, orient * c
            source = cls ^ (4 * abs(a) + 2 * abs(b) + abs(c))
            base = v_row(source, by_z[dc], 0, 1) + by_y[db] + by_x[da]
            block = [
                [stencil_ref[number * 9 + (i * 3 + j if orient == 1 else j * 3 + i)] for j in range(3)]
                for i in range(3)
            ]
            for l in range(L):
                weight = centre[l] + v_ref[pl.ds(base + 3 * 64 + l * 8, 8), :]
                wu = [weight * v_ref[pl.ds(base + j * 64 + l * 8, 8), :] for j in range(3)]
                for i in range(3):
                    term = block[i][0] * wu[0] + block[i][1] * wu[1] + block[i][2] * wu[2]
                    acc[i][l] = term if acc[i][l] is None else acc[i][l] + term
    for l in range(L):
        s = [st_ref[pl.ds(((k * 9 + a) * L + l) * 8, 8), :] for a in range(9)]
        rest = [s[i] - acc[i][l] for i in range(3)]
        inv = ((s[3], s[4], s[5]), (s[4], s[6], s[7]), (s[5], s[7], s[8]))
        for i in range(3):
            v_ref[pl.ds(v_row(cls, 0, i, l + 1), 8), :] = (
                inv[i][0] * rest[0] + inv[i][1] * rest[1] + inv[i][2] * rest[2]
            )
    for i in range(3):
        fill_class(v_ref, cls, pz, i)


def four_colours(r, order_ref, v_ref, st_ref, stencil_ref):
    @pl.loop(0, 4)
    def _(k):
        relax(order_ref[4 * r + k], k, v_ref, st_ref, stencil_ref)


def own_fields(v_ref, f_ref):
    for comp in range(3):
        for l in range(L):
            for p in range(4):
                for px in range(2):
                    f_ref[pl.ds(((comp * L + l) * 4 + p) * 8 + px, 4, stride=2), :] = v_ref[
                        pl.ds(v_row(px * 4 + p, 0, comp, l + 1) + 2, 4), :
                    ]


def clear_pads(v_ref):
    v_ref[pl.ds(0, PAD), :] = jnp.zeros((PAD, 128), F32)
    v_ref[pl.ds(VROWS - PAD, PAD), :] = jnp.zeros((PAD, 128), F32)


VROWS = 2 * PAD + 8 * 2 * 4 * 64
STIFF = 8 * 2 * 64


def first_kernel(
    order_ref, stencil_ref, rl_ref, xl_ref, xr_ref, rr_ref, own_ref, below_ref, above_ref,
    f_ref, lo_ref, hi_ref, stiff_ref, v_ref, e_ref, st_ref,
):
    clear_pads(v_ref)
    fill_fields(4, v_ref, e_ref, rl_ref, xl_ref, xr_ref, rr_ref)
    fill_statics(0, st_ref, rl_ref, xl_ref, xr_ref, rr_ref, own_ref, below_ref, above_ref)
    four_colours(0, order_ref, v_ref, st_ref, stencil_ref)
    own_fields(v_ref, f_ref)
    lowm = low(8)
    for comp in range(3):
        for p in range(4):
            v2 = f_ref[pl.ds(((comp * L + 2) * 4 + p) * 8, 8), :]
            v3 = f_ref[pl.ds(((comp * L + 3) * 4 + p) * 8, 8), :]
            lo_ref[pl.ds((comp * 4 + p) * 8, 8), :] = jnp.where(lowm, v2, swap(v3))
            hi_ref[pl.ds((comp * 4 + p) * 8, 8), :] = jnp.where(lowm, swap(v2), v3)
    for cls in range(8):
        for shifted in range(2):
            stiff_ref[pl.ds((cls * 2 + shifted) * 64, 64), :] = v_ref[pl.ds(v_row(cls, shifted, 3, 0), 64), :]


def second_kernel(
    order_ref, stencil_ref, rl2_ref, xl2_ref, xr2_ref, rr2_ref, stiff_ref,
    rl_ref, xl_ref, xr_ref, rr_ref, own_ref, below_ref, above_ref,
    out_ref, v_ref, e_ref, st_ref, f_ref,
):
    clear_pads(v_ref)
    for cls in range(8):
        for shifted in range(2):
            v_ref[pl.ds(v_row(cls, shifted, 3, 0), 64), :] = stiff_ref[pl.ds((cls * 2 + shifted) * 64, 64), :]
    fill_fields(3, v_ref, e_ref, rl2_ref, xl2_ref, xr2_ref, rr2_ref)
    fill_statics(1, st_ref, rl_ref, xl_ref, xr_ref, rr_ref, own_ref, below_ref, above_ref)
    four_colours(1, order_ref, v_ref, st_ref, stencil_ref)
    own_fields(v_ref, f_ref)
    lowm = low(8)
    lane = lanes(8)
    merge = lax.shift_right_logical(lane, 1) + 64 * (lane & 1)
    for comp in range(3):
        for py in range(2):
            for l in range(L):
                row = ((comp * L + l) * 4 + py * 2) * 8
                ev, od = f_ref[pl.ds(row, 8), :], f_ref[pl.ds(row + 8, 8), :]
                if l >= 2:
                    y = 2 * (l - 2) + py
                    out_ref[pl.ds(comp * 128 + y, 8, stride=16), :] = gather(jnp.where(lowm, ev, swap(od)), merge)
                if l <= 3:
                    y = 2 * (l + 4) + py
                    out_ref[pl.ds(comp * 128 + y, 8, stride=16), :] = gather(jnp.where(lowm, swap(ev), od), merge)


SMEM = pl.BlockSpec(memory_space=pltpu.SMEM)
VMEM = pl.BlockSpec(memory_space=pltpu.VMEM)


def rows_of(*counts):
    return tuple(jax.ShapeDtypeStruct((n, 128), F32) for n in counts)


def call(kernel, specs, outs, scratch, cost):
    return pl.pallas_call(
        kernel,
        in_specs=specs,
        out_shape=rows_of(*outs),
        out_specs=tuple(VMEM for _ in outs),
        scratch_shapes=[pltpu.VMEM((n, 128), F32) for n in scratch],
        compiler_params=pltpu.CompilerParams(vmem_limit_bytes=24 * 1024 * 1024),
        cost_estimate=pl.CostEstimate(flops=cost, bytes_accessed=cost, transcendentals=0),
    )


def ring(value, axis, step):
    count = lax.axis_size(axis)
    return lax.ppermute(value, axis, [(i, (i + step) % count) for i in range(count)])


def per_device(displacement, load_vector, diag_inverse, stiffness, stencil, colour):
    disp = displacement.reshape(3 * 128, 128)
    load = load_vector.reshape(3 * 128, 128)
    inv = diag_inverse.reshape(9 * 128, 128)
    stiff = stiffness.reshape(128, 128)
    corner = colour[:2, :2, :2].reshape(1, 8)
    wanted = jnp.arange(8, dtype=jnp.int32)
    order = jnp.sum(jnp.where(corner == wanted[:, None], wanted[None, :], 0), axis=1)
    coefs = stencil.reshape(117)

    nat = [SMEM] + [VMEM] * 4
    lo, hi = call(pack_y_kernel, nat, (NF + NS, NF + NS), (8, 8), 1 << 20)(order, disp, load, inv, stiff)
    above = ring(lo, "gy", -1)
    below = ring(hi, "gy", 1)
    f, s, own0, own1 = call(convert_kernel, nat, (768, 864, 648, 648), (), 1 << 22)(order, disp, load, inv, stiff)
    xl, xr = call(pack_x_kernel, [VMEM] * 4, (XF + XS, XF + XS), (), 1 << 20)(f, s, below, above)
    rr = ring(xl, "gx", -1)
    rl = ring(xr, "gx", 1)
    f2, lo2, hi2, stiff_v = call(
        first_kernel, [SMEM] * 2 + [VMEM] * 7, (576, 96, 96, STIFF), (VROWS, 384, 1728), 1 << 24
    )(order, coefs, rl, xl, xr, rr, own0, below, above)
    above2 = ring(lo2, "gy", -1)
    below2 = ring(hi2, "gy", 1)
    xl2, xr2 = call(pack_x2_kernel, [VMEM] * 3, (288, 288), (), 1 << 20)(f2, below2, above2)
    rr2 = ring(xl2, "gx", -1)
    rl2 = ring(xr2, "gx", 1)
    (out,) = call(
        second_kernel, [SMEM] * 2 + [VMEM] * 12, (384,), (VROWS, 384, 1728, 576), 1 << 24
    )(order, coefs, rl2, xl2, xr2, rr2, stiff_v, rl, xl, xr, rr, own1, below, above)
    return out.reshape(3, XD, YD, ZD)


def solution(mesh):
    return jax.shard_map(
        per_device,
        mesh=mesh,
        in_specs=(
            P(None, "gx", "gy", None),
            P(None, "gx", "gy", None),
            P(None, None, "gx", "gy", None),
            P("gx", "gy", None),
            P(),
            P("gx", "gy", None),
        ),
        out_specs=P(None, "gx", "gy", None),
        check_vma=False,
    )
```

```python
import jax
import jax.numpy as jnp
from jax import lax
from jax.experimental import pallas as pl
from jax.experimental.pallas import tpu as pltpu
from jax.sharding import PartitionSpec as P

XD, YD, ZD = 8, 16, 128
L = 6
PAD = 8
INV = (0, 1, 2, 4, 5, 8)
F32 = jnp.float32

offsets = [
    (a, b, c)
    for a in (-1, 0, 1)
    for b in (-1, 0, 1)
    for c in (-1, 0, 1)
    if (a, b, c) > (0, 0, 0)
]

NF = 16 * 8
NS = 18 * 8
XF = 4 * L * 4 * 4
XS = 18 * L * 4


def lanes(rows):
    return lax.broadcasted_iota(jnp.int32, (rows, 128), 1)


def low(rows):
    return lanes(rows) < 64


def gather(v, idx):
    return jnp.take_along_axis(v, idx, axis=1, mode="promise_in_bounds")


def split_idx(rows, first):
    lane = lanes(rows)
    return jnp.where(lane < 64, 2 * lane + first, 2 * lane - 127 - first)


def swap(v):
    return pltpu.roll(v, 64, 1)


def parity(cls):
    return lax.shift_right_logical(cls, 2), lax.shift_right_logical(cls, 1) & 1, cls & 1


def load_rows(nat, first, cls_row, y1, count):
    return nat[pl.ds(first + cls_row + 2 * y1, count, stride=32), :]


def static_slices(load_ref, inv_ref):
    return [(load_ref, i * 128) for i in range(3)] + [(inv_ref, i * 128) for i in INV]


def field_slices(disp_ref, stiff_ref):
    return [(disp_ref, 0), (disp_ref, 128), (disp_ref, 256), (stiff_ref, 0)]


def pack_y_kernel(
    colour_hbm, disp_hbm, load_hbm, inv_hbm, stiff_hbm,
    lo_ref, hi_ref, disp_ref, load_ref, inv_ref, stiff_ref, order_ref, near_s, far_s, colour_s, sems,
):
    moves = [
        (colour_hbm.at[pl.ds(0, 8)], colour_s.at[pl.ds(0, 8)]),
        (colour_hbm.at[pl.ds(16, 8)], colour_s.at[pl.ds(8, 8)]),
        (disp_hbm, disp_ref),
        (stiff_hbm, stiff_ref),
        (load_hbm, load_ref),
        (inv_hbm, inv_ref),
    ]
    copies = [pltpu.make_async_copy(a, b, sems.at[i]) for i, (a, b) in enumerate(moves)]
    for copy in copies:
        copy.start()
    copies[0].wait()
    copies[1].wait()
    for cls in range(8):
        px, py, pz = cls >> 2, (cls >> 1) & 1, cls & 1
        order_ref[colour_s[8 * px + py, pz]] = cls
    copies[2].wait()
    copies[3].wait()
    lowm = low(8)
    idx_e = split_idx(8, 0)
    for comp, (ref, first) in enumerate(field_slices(disp_ref, stiff_ref)):
        for py in range(2):
            for out, y1 in ((lo_ref, 0), (hi_ref, 6)):
                a = ref[pl.ds(first + py + 2 * y1, 8, stride=16), :]
                b = ref[pl.ds(first + py + 2 * y1 + 2, 8, stride=16), :]
                if comp == 3:
                    a, b = 0.5 * a, 0.5 * b
                a, b = gather(a, idx_e), gather(b, idx_e)
                row = (comp * 4 + py * 2) * 8
                out[pl.ds(row, 8), :] = jnp.where(lowm, a, swap(b))
                out[pl.ds(row + 8, 8), :] = jnp.where(lowm, swap(a), b)
    copies[4].wait()
    copies[5].wait()
    for r in range(2):
        px, py, pz = zip(*[parity(order_ref[4 * r + k]) for k in range(3)])
        cls_row = [px[k] * 16 + py[k] for k in range(3)]
        for side, out in ((0, lo_ref), (1, hi_ref)):
            near, far = (0, 1) if side == 0 else (7, 6)
            idx_near = [split_idx(4, pz[k] if side == 0 else 1 - pz[k]) for k in range(3)]
            idx_far = [split_idx(4, 1 - pz[k] if side == 0 else pz[k]) for k in range(3)]
            for a, (ref, first) in enumerate(static_slices(load_ref, inv_ref)):
                v = [load_rows(ref, first, cls_row[k], near, 4) for k in range(3)]
                n0 = gather(v[0], idx_near[0])
                f0 = gather(load_rows(ref, first, cls_row[0], far, 4), idx_far[0])
                near_s[0:2, :] = n0[0:2]
                near_s[4:6, :] = n0[2:4]
                far_s[0:2, :] = f0[0:2]
                far_s[4:6, :] = f0[2:4]
                for k in (1, 2):
                    n = gather(v[k], idx_near[k])
                    f = gather(v[k], idx_far[k])
                    near_s[1 + k : 2 + k, :] = n[0:1]
                    near_s[5 + k : 6 + k, :] = n[3:4]
                    far_s[1 + k : 2 + k, :] = f[1:2]
                    far_s[5 + k : 6 + k, :] = f[2:3]
                nv, fv = near_s[...], far_s[...]
                out[pl.ds(NF + (r * 9 + a) * 8, 8), :] = (
                    jnp.where(lowm, nv, fv) if side == 0 else jnp.where(lowm, fv, nv)
                )


def convert_kernel(order_ref, disp_ref, load_ref, inv_ref, stiff_ref, f_ref, s_ref, own0_ref, own1_ref):
    lowm = low(8)
    low4 = low(4)
    idx_e = split_idx(8, 0)
    zero = jnp.zeros((8, 128), F32)
    for comp, (ref, first) in enumerate(field_slices(disp_ref, stiff_ref)):
        for py in range(2):
            ev, od = [], []
            for y1 in range(8):
                v = ref[pl.ds(first + py + 2 * y1, 8, stride=16), :]
                if comp == 3:
                    v = 0.5 * v
                v = gather(v, idx_e)
                ev.append(v)
                od.append(swap(v))
            for l in range(L):
                e0, o0 = (ev[l - 2], od[l - 2]) if l >= 2 else (zero, zero)
                e1, o1 = (ev[l + 4], od[l + 4]) if l <= 3 else (zero, zero)
                row = ((comp * L + l) * 4 + py * 2) * 8
                f_ref[pl.ds(row, 8), :] = jnp.where(lowm, e0, o1)
                f_ref[pl.ds(row + 8, 8), :] = jnp.where(lowm, o0, e1)
    zero4 = jnp.zeros((4, 128), F32)
    for r, own in ((0, own0_ref), (1, own1_ref)):
        for k in range(4):
            px, py, pz = parity(order_ref[4 * r + k])
            cls_row = px * 16 + py
            idx0, idx1 = split_idx(4, pz), split_idx(4, 1 - pz)
            for a, (ref, first) in enumerate(static_slices(load_ref, inv_ref)):
                rows = [load_rows(ref, first, cls_row, y1, 4) for y1 in range(8)]
                for l in range(L):
                    v0 = gather(rows[l - 2], idx0) if l >= 2 else zero4
                    v1 = gather(rows[l + 4], idx1) if l <= 3 else zero4
                    v = jnp.where(low4, v0, v1)
                    srow = ((r * 9 + a) * L + l) * 8
                    if k == 0:
                        s_ref[pl.ds(srow, 2), :] = v[0:2]
                        s_ref[pl.ds(srow + 4, 2), :] = v[2:4]
                    else:
                        own[pl.ds((((k - 1) * 9 + a) * L + l) * 4, 4), :] = v
                        if k < 3:
                            s_ref[pl.ds(srow + 1 + k, 1), :] = v[0:1]
                            s_ref[pl.ds(srow + 5 + k, 1), :] = v[3:4]


def add_y(v, l, below, above, lowm):
    if l == 0:
        return jnp.where(lowm, below, v)
    if l == 1:
        return jnp.where(lowm, swap(below), v)
    if l == 4:
        return jnp.where(lowm, v, swap(above))
    if l == 5:
        return jnp.where(lowm, v, above)
    return v


def put_pair(xl_ref, xr_ref, row, v, w):
    sub = lax.broadcasted_iota(jnp.int32, (8, 128), 0) < 4
    xl_ref[pl.ds(row, 8), :] = jnp.where(sub, v, pltpu.roll(w, 4, 0))
    xr_ref[pl.ds(row, 8), :] = jnp.where(sub, pltpu.roll(v, 4, 0), w)


def y_masks():
    gy = lax.axis_index("gy")
    return (
        jnp.where(gy > 0, 1.0, 0.0).astype(F32),
        jnp.where(gy < lax.axis_size("gy") - 1, 1.0, 0.0).astype(F32),
    )


def x_masks():
    gx = lax.axis_index("gx")
    return (
        jnp.where(gx > 0, 1.0, 0.0).astype(F32),
        jnp.where(gx < lax.axis_size("gx") - 1, 1.0, 0.0).astype(F32),
    )


def pack_x_fields(comps, f_ref, below_ref, above_ref, xl_ref, xr_ref):
    lowm = low(8)
    m_below, m_above = y_masks()
    for comp in range(comps):
        for half in range(2):
            below = [below_ref[pl.ds((comp * 4 + 2 * half + i) * 8, 8), :] * m_below for i in range(2)]
            above = [above_ref[pl.ds((comp * 4 + 2 * half + i) * 8, 8), :] * m_above for i in range(2)]
            for l in range(L):
                row = (comp * L + l) * 4 + 2 * half
                v = [add_y(f_ref[pl.ds((row + i) * 8, 8), :], l, below[i], above[i], lowm) for i in range(2)]
                put_pair(xl_ref, xr_ref, row * 4, v[0], v[1])


def pack_x_kernel(f_ref, s_ref, below_ref, above_ref, xl_ref, xr_ref):
    pack_x_fields(4, f_ref, below_ref, above_ref, xl_ref, xr_ref)
    lowm = low(8)
    m_below, m_above = y_masks()
    for ra in range(18):
        below = below_ref[pl.ds(NF + ra * 8, 8), :] * m_below
        above = above_ref[pl.ds(NF + ra * 8, 8), :] * m_above
        for l in range(0, L, 2):
            row = ra * L + l
            v = [add_y(s_ref[pl.ds((row + i) * 8, 8), :], l + i, below, above, lowm) for i in range(2)]
            put_pair(xl_ref, xr_ref, XF + row * 4, v[0], v[1])


def pack_x2_kernel(f_ref, below_ref, above_ref, xl_ref, xr_ref):
    pack_x_fields(3, f_ref, below_ref, above_ref, xl_ref, xr_ref)


def v_row(cls, shifted, comp, ext):
    return PAD + (((cls * 2 + shifted) * 4 + comp) * 8 + ext) * 8


def fill_class(v_ref, cls, pz, comp, v):
    low_edge = pz == 1
    if isinstance(pz, int):
        shift, edge = (1, 0) if low_edge else (127, 63)
        shift_swap = (shift + 64) % 128
    else:
        shift, edge = jnp.where(low_edge, 1, 127), jnp.where(low_edge, 0, 63)
        shift_swap = jnp.where(low_edge, 65, 63)
    keep = (lanes(8) & 63) != edge
    base = v_row(cls, 0, comp, 0)
    moved = v_row(cls, 1, comp, 0)
    for l in (0, L - 1):
        ext = 56 if l == 0 else 0
        v_ref[pl.ds(base + ext, 8), :] = swap(v[l])
        v_ref[pl.ds(moved + ext, 8), :] = jnp.where(keep, pltpu.roll(v[l], shift_swap, 1), 0.0)
    for l in range(L):
        v_ref[pl.ds(moved + (l + 1) * 8, 8), :] = jnp.where(keep, pltpu.roll(v[l], shift, 1), 0.0)


def fill_all(comps, v_ref):
    for comp in range(comps):
        for cls in range(8):
            base = v_row(cls, 0, comp, 1)
            fill_class(v_ref, cls, cls & 1, comp, [v_ref[pl.ds(base + l * 8, 8), :] for l in range(L)])


def place_own(comps, v_ref, e_ref, xl_ref, xr_ref):
    zero = jnp.zeros((8, 128), F32)
    sub = lax.broadcasted_iota(jnp.int32, (8, 128), 0) < 4
    for comp in range(comps):
        for l in range(L):
            for p in (0, 2):
                row = ((comp * L + l) * 4 + p) * 4
                a, b = xl_ref[pl.ds(row, 8), :], xr_ref[pl.ds(row, 8), :]
                at = (l * 4 + p) * 16
                e_ref[pl.ds(at + 4, 8), :] = jnp.where(sub, a, pltpu.roll(b, 4, 0))
                e_ref[pl.ds(at + 20, 8), :] = jnp.where(sub, pltpu.roll(a, 4, 0), b)
        for l in range(L):
            for p in range(4):
                for px in range(2):
                    v_ref[pl.ds(v_row(px * 4 + p, 0, comp, l + 1), 8), :] = e_ref[
                        pl.ds((l * 4 + p) * 16 + px, 8, stride=2), :
                    ]


def place_ghosts(comps, v_ref, rl_ref, rr_ref):
    m_left, m_right = x_masks()
    for comp in range(comps):
        for p in range(4):
            for px in range(2):
                base = v_row(px * 4 + p, 0, comp, 1)
                for i in range(2):
                    row = (comp * L * 4 + p) * 4 + px + 2 * i
                    v_ref[pl.ds(base + i, L, stride=8), :] = rl_ref[pl.ds(row, L, stride=16), :] * m_left
                    v_ref[pl.ds(base + 6 + i, L, stride=8), :] = rr_ref[pl.ds(row, L, stride=16), :] * m_right


def place_own_statics(r, st_ref, xl_ref, xr_ref, own_ref, below_ref, above_ref):
    m_below, m_above = y_masks()
    lowm = low(1)
    zero = jnp.zeros((8, 128), F32)
    for a in range(9):
        below = below_ref[pl.ds(NF + (r * 9 + a) * 8, 8), :] * m_below
        above = above_ref[pl.ds(NF + (r * 9 + a) * 8, 8), :] * m_above
        for l in range(L):
            srow = XF + ((r * 9 + a) * L + l) * 4
            own_l, own_r = xl_ref[pl.ds(srow, 4), :], xr_ref[pl.ds(srow, 4), :]
            at = (a * L + l) * 8
            st_ref[pl.ds(at, 8), :] = zero
            st_ref[pl.ds(at + 2, 2), :] = own_l[0:2]
            st_ref[pl.ds(at + 4, 2), :] = own_r[0:2]
            for k in (1, 2, 3):
                at = ((k * 9 + a) * L + l) * 8
                st_ref[pl.ds(at, 8), :] = zero
                st_ref[pl.ds(at + 2, 4), :] = own_ref[pl.ds((((k - 1) * 9 + a) * L + l) * 4, 4), :]
                if k < 3:
                    st_ref[pl.ds(at + 2, 1), :] = own_l[1 + k : 2 + k]
                    st_ref[pl.ds(at + 5, 1), :] = own_r[1 + k : 2 + k]
                    for q in range(2):
                        at_q = at + 3 + q
                        if l == 1:
                            st_ref[pl.ds(at_q, 1), :] = jnp.where(
                                lowm, below[1 + k + 4 * q : 2 + k + 4 * q], st_ref[pl.ds(at_q, 1), :]
                            )
                        if l == 4:
                            st_ref[pl.ds(at_q, 1), :] = jnp.where(
                                lowm, st_ref[pl.ds(at_q, 1), :], above[1 + k + 4 * q : 2 + k + 4 * q]
                            )


def place_ghost_statics(r, st_ref, rl_ref, rr_ref):
    m_left, m_right = x_masks()
    for a in range(9):
        for row, k, at_l, at_r in ((0, 0, 0, 6), (1, 0, 1, 7), (2, 1, 1, 6), (3, 2, 1, 6)):
            src = pl.ds(XF + (r * 9 + a) * L * 4 + row, L, stride=4)
            base = (k * 9 + a) * L * 8
            st_ref[pl.ds(base + at_l, L, stride=8), :] = rl_ref[src, :] * m_left
            st_ref[pl.ds(base + at_r, L, stride=8), :] = rr_ref[src, :] * m_right


def relax(cls, k, v_ref, st_ref, stencil_ref):
    px, py, pz = parity(cls)
    by_x = {0: 0, -1: px - 1, 1: px}
    by_y = {0: 0, -1: (py - 1) * 8, 1: py * 8}
    by_z = {0: 0, -1: 1 - pz, 1: pz}
    centre = [v_ref[pl.ds(v_row(cls, 0, 3, l + 1), 8), :] for l in range(L)]
    acc = [[None] * L for _ in range(3)]
    fresh = [[None] * L for _ in range(3)]
    for number, (a, b, c) in enumerate(offsets):
        for orient in (1, -1):
            da, db, dc = orient * a, orient * b, orient * c
            source = cls ^ (4 * abs(a) + 2 * abs(b) + abs(c))
            base = v_row(source, by_z[dc], 0, 1) + by_y[db] + by_x[da]
            block = [
                [stencil_ref[number * 9 + (i * 3 + j if orient == 1 else j * 3 + i)] for j in range(3)]
                for i in range(3)
            ]
            for l in range(L):
                weight = centre[l] + v_ref[pl.ds(base + 3 * 64 + l * 8, 8), :]
                wu = [weight * v_ref[pl.ds(base + j * 64 + l * 8, 8), :] for j in range(3)]
                for i in range(3):
                    term = block[i][0] * wu[0] + block[i][1] * wu[1] + block[i][2] * wu[2]
                    acc[i][l] = term if acc[i][l] is None else acc[i][l] + term
    for l in range(L):
        s = [st_ref[pl.ds(((k * 9 + a) * L + l) * 8, 8), :] for a in range(9)]
        rest = [s[i] - acc[i][l] for i in range(3)]
        inv = ((s[3], s[4], s[5]), (s[4], s[6], s[7]), (s[5], s[7], s[8]))
        for i in range(3):
            fresh[i][l] = inv[i][0] * rest[0] + inv[i][1] * rest[1] + inv[i][2] * rest[2]
            v_ref[pl.ds(v_row(cls, 0, i, l + 1), 8), :] = fresh[i][l]

    @pl.when(k < 3)
    def _():
        for i in range(3):
            fill_class(v_ref, cls, pz, i, fresh[i])


def four_colours(r, order_ref, v_ref, st_ref, stencil_ref):
    @pl.loop(0, 4)
    def _(k):
        relax(order_ref[4 * r + k], k, v_ref, st_ref, stencil_ref)


VROWS = 2 * PAD + 8 * 2 * 4 * 64
STROWS = 4 * 9 * L * 8


def prepare_kernel(xl_ref, xr_ref, own_ref, below_ref, above_ref, v_ref, st_ref, e_ref):
    v_ref[pl.ds(0, PAD), :] = jnp.zeros((PAD, 128), F32)
    v_ref[pl.ds(VROWS - PAD, PAD), :] = jnp.zeros((PAD, 128), F32)
    place_own(4, v_ref, e_ref, xl_ref, xr_ref)
    place_own_statics(0, st_ref, xl_ref, xr_ref, own_ref, below_ref, above_ref)


def first_kernel(order_ref, stencil_ref, rl_ref, rr_ref, _v, _st, v_ref, st_ref, lo_ref, hi_ref):
    place_ghosts(4, v_ref, rl_ref, rr_ref)
    place_ghost_statics(0, st_ref, rl_ref, rr_ref)
    fill_all(4, v_ref)
    four_colours(0, order_ref, v_ref, st_ref, stencil_ref)
    lowm = low(4)
    for comp in range(3):
        for p in range(4):
            for px in range(2):
                at = v_row(px * 4 + p, 0, comp, 3) + 2
                v2, v3 = v_ref[pl.ds(at, 4), :], v_ref[pl.ds(at + 8, 4), :]
                to = pl.ds((comp * 4 + p) * 8 + px, 4, stride=2)
                lo_ref[to, :] = jnp.where(lowm, v2, swap(v3))
                hi_ref[to, :] = jnp.where(lowm, swap(v2), v3)


def between_kernel(v_ref, rl_ref, xl_ref, xr_ref, rr_ref, own_ref, below_ref, above_ref, f_ref, st_ref):
    for comp in range(3):
        for l in range(L):
            for p in range(4):
                for px in range(2):
                    f_ref[pl.ds(((comp * L + l) * 4 + p) * 8 + px, 4, stride=2), :] = v_ref[
                        pl.ds(v_row(px * 4 + p, 0, comp, l + 1) + 2, 4), :
                    ]
    place_own_statics(1, st_ref, xl_ref, xr_ref, own_ref, below_ref, above_ref)
    place_ghost_statics(1, st_ref, rl_ref, rr_ref)


def prepare2_kernel(xl_ref, xr_ref, _v, v_ref, e_ref):
    place_own(3, v_ref, e_ref, xl_ref, xr_ref)


def second_kernel(order_ref, stencil_ref, rl_ref, rr_ref, st_ref, _v, out_ref, v_ref):
    place_ghosts(3, v_ref, rl_ref, rr_ref)
    fill_all(3, v_ref)
    four_colours(1, order_ref, v_ref, st_ref, stencil_ref)
    lowm = low(8)
    lane = lanes(8)
    merge = lax.shift_right_logical(lane, 1) + 64 * (lane & 1)
    for comp in range(3):
        for px in range(2):
            for py in range(2):
                cls = px * 4 + py * 2
                for l in range(L):
                    ev = v_ref[pl.ds(v_row(cls, 0, comp, l + 1), 8), :]
                    od = v_ref[pl.ds(v_row(cls + 1, 0, comp, l + 1), 8), :]
                    first = comp * 128 + px * 16 + py
                    if l >= 2:
                        out_ref[pl.ds(first + 2 * (l - 2), 4, stride=32), :] = gather(
                            jnp.where(lowm, ev, swap(od)), merge
                        )[2:6]
                    if l <= 3:
                        out_ref[pl.ds(first + 2 * (l + 4), 4, stride=32), :] = gather(
                            jnp.where(lowm, swap(ev), od), merge
                        )[2:6]


SMEM = pl.BlockSpec(memory_space=pltpu.SMEM)
VMEM = pl.BlockSpec(memory_space=pltpu.VMEM)


HBM = pl.BlockSpec(memory_space=pltpu.HBM)


def call(kernel, specs, outs, scratch, cost, aliases={}, extra_outs=(), extra_out_specs=(), extra_scratch=()):
    return pl.pallas_call(
        kernel,
        in_specs=specs,
        out_shape=tuple(jax.ShapeDtypeStruct((n, 128), F32) for n in outs) + tuple(extra_outs),
        out_specs=tuple(VMEM for _ in outs) + tuple(extra_out_specs),
        scratch_shapes=[pltpu.VMEM((n, 128), F32) for n in scratch] + list(extra_scratch),
        input_output_aliases=aliases,
        compiler_params=pltpu.CompilerParams(vmem_limit_bytes=24 * 1024 * 1024),
        cost_estimate=pl.CostEstimate(flops=cost, bytes_accessed=cost, transcendentals=0),
    )


def ring(value, axis, step):
    count = lax.axis_size(axis)
    return lax.ppermute(value, axis, [(i, (i + step) % count) for i in range(count)])


def per_device(displacement, load_vector, diag_inverse, stiffness, stencil, colour):
    disp = displacement.reshape(3 * 128, 128)
    load = load_vector.reshape(3 * 128, 128)
    inv = diag_inverse.reshape(9 * 128, 128)
    stiff = stiffness.reshape(128, 128)
    colours = colour.reshape(128, 128)
    coefs = stencil.reshape(117)

    lo, hi, disp, load, inv, stiff, order = call(
        pack_y_kernel,
        [HBM] * 5,
        (NF + NS, NF + NS, 384, 384, 1152, 128),
        (8, 8),
        1 << 20,
        extra_outs=[jax.ShapeDtypeStruct((8,), jnp.int32)],
        extra_out_specs=[SMEM],
        extra_scratch=[pltpu.SMEM((16, 128), jnp.int32), pltpu.SemaphoreType.DMA((6,))],
    )(colours, disp, load, inv, stiff)
    above = ring(lo, "gy", -1)
    below = ring(hi, "gy", 1)
    f, s, own0, own1 = call(convert_kernel, [SMEM] + [VMEM] * 4, (768, 864, 648, 648), (), 1 << 22)(
        order, disp, load, inv, stiff
    )
    xl, xr = call(pack_x_kernel, [VMEM] * 4, (XF + XS, XF + XS), (), 1 << 20)(f, s, below, above)
    rr = ring(xl, "gx", -1)
    rl = ring(xr, "gx", 1)
    v, st = call(prepare_kernel, [VMEM] * 5, (VROWS, STROWS), (384,), 1 << 22)(xl, xr, own0, below, above)
    v, _, lo2, hi2 = call(
        first_kernel, [SMEM] * 2 + [VMEM] * 4, (VROWS, STROWS, 96, 96), (), 1 << 24, aliases={4: 0, 5: 1}
    )(order, coefs, rl, rr, v, st)
    above2 = ring(lo2, "gy", -1)
    below2 = ring(hi2, "gy", 1)
    f2, st = call(between_kernel, [VMEM] * 8, (576, STROWS), (), 1 << 22)(v, rl, xl, xr, rr, own1, below, above)
    xl2, xr2 = call(pack_x2_kernel, [VMEM] * 3, (288, 288), (), 1 << 20)(f2, below2, above2)
    rr2 = ring(xl2, "gx", -1)
    rl2 = ring(xr2, "gx", 1)
    (v,) = call(prepare2_kernel, [VMEM] * 3, (VROWS,), (384,), 1 << 22, aliases={2: 0})(xl2, xr2, v)
    out, _ = call(second_kernel, [SMEM] * 2 + [VMEM] * 4, (384, VROWS), (), 1 << 24, aliases={5: 1})(
        order, coefs, rl2, rr2, st, v
    )
    return out.reshape(3, XD, YD, ZD)


def solution(mesh):
    return jax.shard_map(
        per_device,
        mesh=mesh,
        in_specs=(
            P(None, "gx", "gy", None),
            P(None, "gx", "gy", None),
            P(None, None, "gx", "gy", None),
            P("gx", "gy", None),
            P(),
            P("gx", "gy", None),
        ),
        out_specs=P(None, "gx", "gy", None),
        check_vma=False,
    )
```

```python
import jax
import jax.numpy as jnp
from jax import lax
from jax.experimental import pallas as pl
from jax.experimental.pallas import tpu as pltpu
from jax.sharding import PartitionSpec as P

XD, YD, ZD = 8, 16, 128
L = 6
PAD = 8
F32 = jnp.float32

offsets = [
    (a, b, c)
    for a in (-1, 0, 1)
    for b in (-1, 0, 1)
    for c in (-1, 0, 1)
    if (a, b, c) > (0, 0, 0)
]

NF = 16 * 8
NS = 18 * 8
XF = 4 * L * 4 * 4
XS = 18 * L * 4


def lanes(rows):
    return lax.broadcasted_iota(jnp.int32, (rows, 128), 1)


def low(rows):
    return lanes(rows) < 64


def gather(v, idx):
    return jnp.take_along_axis(v, idx, axis=1, mode="promise_in_bounds")


def split_idx(rows, first):
    lane = lanes(rows)
    return jnp.where(lane < 64, 2 * lane + first, 2 * lane - 127 - first)


def swap(v):
    return pltpu.roll(v, 64, 1)


def parity(cls):
    return lax.shift_right_logical(cls, 2), lax.shift_right_logical(cls, 1) & 1, cls & 1


def load_rows(nat, first, cls_row, y1, count):
    return nat[pl.ds(first + cls_row + 2 * y1, count, stride=32), :]


NAT_LOAD, NAT_INV, NAT_STIFF, NAT_ORDER, NAT_ROWS = 384, 768, 1536, 1664, 1672


def static_rows():
    return [NAT_LOAD + i * 128 for i in range(3)] + [NAT_INV + i * 128 for i in range(6)]


def field_rows():
    return [0, 128, 256, NAT_STIFF]


def pack_y_kernel(
    colour_hbm, disp_hbm, load_hbm, inv_hbm, stiff_hbm,
    lo_ref, hi_ref, order_ref, nat_hbm, nat_ref, near_s, far_s, colour_s, sems,
):
    moves = [
        (colour_hbm.at[pl.ds(0, 8)], colour_s.at[pl.ds(0, 8)]),
        (colour_hbm.at[pl.ds(16, 8)], colour_s.at[pl.ds(8, 8)]),
        (disp_hbm, nat_ref.at[pl.ds(0, 384)]),
        (stiff_hbm, nat_ref.at[pl.ds(NAT_STIFF, 128)]),
        (load_hbm, nat_ref.at[pl.ds(NAT_LOAD, 384)]),
        (inv_hbm.at[pl.ds(0, 384)], nat_ref.at[pl.ds(NAT_INV, 384)]),
        (inv_hbm.at[pl.ds(512, 256)], nat_ref.at[pl.ds(NAT_INV + 384, 256)]),
        (inv_hbm.at[pl.ds(1024, 128)], nat_ref.at[pl.ds(NAT_INV + 640, 128)]),
    ]
    copies = [pltpu.make_async_copy(a, b, sems.at[i]) for i, (a, b) in enumerate(moves)]
    for copy in copies:
        copy.start()
    copies[0].wait()
    copies[1].wait()
    for cls in range(8):
        px, py, pz = cls >> 2, (cls >> 1) & 1, cls & 1
        order_ref[colour_s[8 * px + py, pz]] = cls
    for k in range(8):
        nat_ref[pl.ds(NAT_ORDER + k, 1), :] = jnp.full((1, 128), order_ref[k].astype(F32))
    copies[2].wait()
    copies[3].wait()
    lowm = low(8)
    idx_e = split_idx(8, 0)
    for comp, first in enumerate(field_rows()):
        for py in range(2):
            for out, y1 in ((lo_ref, 0), (hi_ref, 6)):
                a = nat_ref[pl.ds(first + py + 2 * y1, 8, stride=16), :]
                b = nat_ref[pl.ds(first + py + 2 * y1 + 2, 8, stride=16), :]
                if comp == 3:
                    a, b = 0.5 * a, 0.5 * b
                a, b = gather(a, idx_e), gather(b, idx_e)
                row = (comp * 4 + py * 2) * 8
                out[pl.ds(row, 8), :] = jnp.where(lowm, a, swap(b))
                out[pl.ds(row + 8, 8), :] = jnp.where(lowm, swap(a), b)
    for copy in copies[4:]:
        copy.wait()
    keep = pltpu.make_async_copy(nat_ref, nat_hbm, sems.at[8])
    keep.start()
    for r in range(2):
        px, py, pz = zip(*[parity(order_ref[4 * r + k]) for k in range(3)])
        cls_row = [px[k] * 16 + py[k] for k in range(3)]
        for side, out in ((0, lo_ref), (1, hi_ref)):
            near, far = (0, 1) if side == 0 else (7, 6)
            idx_near = [split_idx(4, pz[k] if side == 0 else 1 - pz[k]) for k in range(3)]
            idx_far = [split_idx(4, 1 - pz[k] if side == 0 else pz[k]) for k in range(3)]
            for a, first in enumerate(static_rows()):
                v = [load_rows(nat_ref, first, cls_row[k], near, 4) for k in range(3)]
                n0 = gather(v[0], idx_near[0])
                f0 = gather(load_rows(nat_ref, first, cls_row[0], far, 4), idx_far[0])
                near_s[0:2, :] = n0[0:2]
                near_s[4:6, :] = n0[2:4]
                far_s[0:2, :] = f0[0:2]
                far_s[4:6, :] = f0[2:4]
                for k in (1, 2):
                    n = gather(v[k], idx_near[k])
                    f = gather(v[k], idx_far[k])
                    near_s[1 + k : 2 + k, :] = n[0:1]
                    near_s[5 + k : 6 + k, :] = n[3:4]
                    far_s[1 + k : 2 + k, :] = f[1:2]
                    far_s[5 + k : 6 + k, :] = f[2:3]
                nv, fv = near_s[...], far_s[...]
                out[pl.ds(NF + (r * 9 + a) * 8, 8), :] = (
                    jnp.where(lowm, nv, fv) if side == 0 else jnp.where(lowm, fv, nv)
                )
    keep.wait()


def convert_kernel(nat_ref, f_ref, s_ref, own0_ref, own1_ref):
    lowm = low(8)
    low4 = low(4)
    idx_e = split_idx(8, 0)
    zero = jnp.zeros((8, 128), F32)
    for comp, first in enumerate(field_rows()):
        for py in range(2):
            ev, od = [], []
            for y1 in range(8):
                v = nat_ref[pl.ds(first + py + 2 * y1, 8, stride=16), :]
                if comp == 3:
                    v = 0.5 * v
                v = gather(v, idx_e)
                ev.append(v)
                od.append(swap(v))
            for l in range(L):
                e0, o0 = (ev[l - 2], od[l - 2]) if l >= 2 else (zero, zero)
                e1, o1 = (ev[l + 4], od[l + 4]) if l <= 3 else (zero, zero)
                row = ((comp * L + l) * 4 + py * 2) * 8
                f_ref[pl.ds(row, 8), :] = jnp.where(lowm, e0, o1)
                f_ref[pl.ds(row + 8, 8), :] = jnp.where(lowm, o0, e1)
    zero4 = jnp.zeros((4, 128), F32)
    for r, own in ((0, own0_ref), (1, own1_ref)):
        for k in range(4):
            px, py, pz = parity(nat_ref[NAT_ORDER + 4 * r + k, 0].astype(jnp.int32))
            cls_row = px * 16 + py
            idx0, idx1 = split_idx(4, pz), split_idx(4, 1 - pz)
            for a, first in enumerate(static_rows()):
                rows = [load_rows(nat_ref, first, cls_row, y1, 4) for y1 in range(8)]
                for l in range(L):
                    v0 = gather(rows[l - 2], idx0) if l >= 2 else zero4
                    v1 = gather(rows[l + 4], idx1) if l <= 3 else zero4
                    v = jnp.where(low4, v0, v1)
                    srow = ((r * 9 + a) * L + l) * 8
                    if k == 0:
                        s_ref[pl.ds(srow, 2), :] = v[0:2]
                        s_ref[pl.ds(srow + 4, 2), :] = v[2:4]
                    else:
                        own[pl.ds((((k - 1) * 9 + a) * L + l) * 4, 4), :] = v
                        if k < 3:
                            s_ref[pl.ds(srow + 1 + k, 1), :] = v[0:1]
                            s_ref[pl.ds(srow + 5 + k, 1), :] = v[3:4]


def add_y(v, l, below, above, lowm):
    if l == 0:
        return jnp.where(lowm, below, v)
    if l == 1:
        return jnp.where(lowm, swap(below), v)
    if l == 4:
        return jnp.where(lowm, v, swap(above))
    if l == 5:
        return jnp.where(lowm, v, above)
    return v


def put_pair(xl_ref, xr_ref, row, v, w):
    sub = lax.broadcasted_iota(jnp.int32, (8, 128), 0) < 4
    xl_ref[pl.ds(row, 8), :] = jnp.where(sub, v, pltpu.roll(w, 4, 0))
    xr_ref[pl.ds(row, 8), :] = jnp.where(sub, pltpu.roll(v, 4, 0), w)


def y_masks():
    gy = lax.axis_index("gy")
    return (
        jnp.where(gy > 0, 1.0, 0.0).astype(F32),
        jnp.where(gy < lax.axis_size("gy") - 1, 1.0, 0.0).astype(F32),
    )


def x_masks():
    gx = lax.axis_index("gx")
    return (
        jnp.where(gx > 0, 1.0, 0.0).astype(F32),
        jnp.where(gx < lax.axis_size("gx") - 1, 1.0, 0.0).astype(F32),
    )


def pack_x_fields(comps, f_ref, below_ref, above_ref, xl_ref, xr_ref):
    lowm = low(8)
    m_below, m_above = y_masks()
    for comp in range(comps):
        for half in range(2):
            below = [below_ref[pl.ds((comp * 4 + 2 * half + i) * 8, 8), :] * m_below for i in range(2)]
            above = [above_ref[pl.ds((comp * 4 + 2 * half + i) * 8, 8), :] * m_above for i in range(2)]
            for l in range(L):
                row = (comp * L + l) * 4 + 2 * half
                v = [add_y(f_ref[pl.ds((row + i) * 8, 8), :], l, below[i], above[i], lowm) for i in range(2)]
                put_pair(xl_ref, xr_ref, row * 4, v[0], v[1])


def pack_x_kernel(f_ref, s_ref, below_ref, above_ref, xl_ref, xr_ref):
    pack_x_fields(4, f_ref, below_ref, above_ref, xl_ref, xr_ref)
    lowm = low(8)
    m_below, m_above = y_masks()
    for ra in range(18):
        below = below_ref[pl.ds(NF + ra * 8, 8), :] * m_below
        above = above_ref[pl.ds(NF + ra * 8, 8), :] * m_above
        for l in range(0, L, 2):
            row = ra * L + l
            v = [add_y(s_ref[pl.ds((row + i) * 8, 8), :], l + i, below, above, lowm) for i in range(2)]
            put_pair(xl_ref, xr_ref, XF + row * 4, v[0], v[1])


def pack_x2_kernel(f_ref, below_ref, above_ref, xl_ref, xr_ref):
    pack_x_fields(3, f_ref, below_ref, above_ref, xl_ref, xr_ref)


def v_row(cls, shifted, comp, ext):
    return PAD + (((cls * 2 + shifted) * 4 + comp) * 8 + ext) * 8


def fill_class(v_ref, cls, pz, comp, v):
    low_edge = pz == 1
    if isinstance(pz, int):
        shift, edge = (1, 0) if low_edge else (127, 63)
        shift_swap = (shift + 64) % 128
    else:
        shift, edge = jnp.where(low_edge, 1, 127), jnp.where(low_edge, 0, 63)
        shift_swap = jnp.where(low_edge, 65, 63)
    keep = (lanes(8) & 63) != edge
    base = v_row(cls, 0, comp, 0)
    moved = v_row(cls, 1, comp, 0)
    for l in (0, L - 1):
        ext = 56 if l == 0 else 0
        v_ref[pl.ds(base + ext, 8), :] = swap(v[l])
        v_ref[pl.ds(moved + ext, 8), :] = jnp.where(keep, pltpu.roll(v[l], shift_swap, 1), 0.0)
    for l in range(L):
        v_ref[pl.ds(moved + (l + 1) * 8, 8), :] = jnp.where(keep, pltpu.roll(v[l], shift, 1), 0.0)


def fill_all(comps, v_ref):
    for comp in range(comps):
        for cls in range(8):
            base = v_row(cls, 0, comp, 1)
            fill_class(v_ref, cls, cls & 1, comp, [v_ref[pl.ds(base + l * 8, 8), :] for l in range(L)])


def place_own(comps, v_ref, e_ref, xl_ref, xr_ref):
    zero = jnp.zeros((8, 128), F32)
    sub = lax.broadcasted_iota(jnp.int32, (8, 128), 0) < 4
    for comp in range(comps):
        for l in range(L):
            for p in (0, 2):
                row = ((comp * L + l) * 4 + p) * 4
                a, b = xl_ref[pl.ds(row, 8), :], xr_ref[pl.ds(row, 8), :]
                at = (l * 4 + p) * 16
                e_ref[pl.ds(at + 4, 8), :] = jnp.where(sub, a, pltpu.roll(b, 4, 0))
                e_ref[pl.ds(at + 20, 8), :] = jnp.where(sub, pltpu.roll(a, 4, 0), b)
        for l in range(L):
            for p in range(4):
                for px in range(2):
                    v_ref[pl.ds(v_row(px * 4 + p, 0, comp, l + 1), 8), :] = e_ref[
                        pl.ds((l * 4 + p) * 16 + px, 8, stride=2), :
                    ]


def place_ghosts(comps, v_ref, rl_ref, rr_ref):
    m_left, m_right = x_masks()
    for comp in range(comps):
        for p in range(4):
            for px in range(2):
                base = v_row(px * 4 + p, 0, comp, 1)
                for i in range(2):
                    row = (comp * L * 4 + p) * 4 + px + 2 * i
                    v_ref[pl.ds(base + i, L, stride=8), :] = rl_ref[pl.ds(row, L, stride=16), :] * m_left
                    v_ref[pl.ds(base + 6 + i, L, stride=8), :] = rr_ref[pl.ds(row, L, stride=16), :] * m_right


def place_own_statics(r, st_ref, xl_ref, xr_ref, own_ref, below_ref, above_ref):
    m_below, m_above = y_masks()
    lowm = low(1)
    zero = jnp.zeros((8, 128), F32)
    for a in range(9):
        below = below_ref[pl.ds(NF + (r * 9 + a) * 8, 8), :] * m_below
        above = above_ref[pl.ds(NF + (r * 9 + a) * 8, 8), :] * m_above
        for l in range(L):
            srow = XF + ((r * 9 + a) * L + l) * 4
            own_l, own_r = xl_ref[pl.ds(srow, 4), :], xr_ref[pl.ds(srow, 4), :]
            at = (a * L + l) * 8
            st_ref[pl.ds(at, 8), :] = zero
            st_ref[pl.ds(at + 2, 2), :] = own_l[0:2]
            st_ref[pl.ds(at + 4, 2), :] = own_r[0:2]
            for k in (1, 2, 3):
                at = ((k * 9 + a) * L + l) * 8
                st_ref[pl.ds(at, 8), :] = zero
                st_ref[pl.ds(at + 2, 4), :] = own_ref[pl.ds((((k - 1) * 9 + a) * L + l) * 4, 4), :]
                if k < 3:
                    st_ref[pl.ds(at + 2, 1), :] = own_l[1 + k : 2 + k]
                    st_ref[pl.ds(at + 5, 1), :] = own_r[1 + k : 2 + k]
                    for q in range(2):
                        at_q = at + 3 + q
                        if l == 1:
                            st_ref[pl.ds(at_q, 1), :] = jnp.where(
                                lowm, below[1 + k + 4 * q : 2 + k + 4 * q], st_ref[pl.ds(at_q, 1), :]
                            )
                        if l == 4:
                            st_ref[pl.ds(at_q, 1), :] = jnp.where(
                                lowm, st_ref[pl.ds(at_q, 1), :], above[1 + k + 4 * q : 2 + k + 4 * q]
                            )


def place_ghost_statics(r, st_ref, rl_ref, rr_ref):
    m_left, m_right = x_masks()
    for a in range(9):
        for row, k, at_l, at_r in ((0, 0, 0, 6), (1, 0, 1, 7), (2, 1, 1, 6), (3, 2, 1, 6)):
            src = pl.ds(XF + (r * 9 + a) * L * 4 + row, L, stride=4)
            base = (k * 9 + a) * L * 8
            st_ref[pl.ds(base + at_l, L, stride=8), :] = rl_ref[src, :] * m_left
            st_ref[pl.ds(base + at_r, L, stride=8), :] = rr_ref[src, :] * m_right


def relax(cls, k, v_ref, st_ref, stencil_ref):
    px, py, pz = parity(cls)
    by_x = {0: 0, -1: px - 1, 1: px}
    by_y = {0: 0, -1: (py - 1) * 8, 1: py * 8}
    by_z = {0: 0, -1: 1 - pz, 1: pz}
    centre = [v_ref[pl.ds(v_row(cls, 0, 3, l + 1), 8), :] for l in range(L)]
    acc = [[None] * L for _ in range(3)]
    fresh = [[None] * L for _ in range(3)]
    for number, (a, b, c) in enumerate(offsets):
        for orient in (1, -1):
            da, db, dc = orient * a, orient * b, orient * c
            source = cls ^ (4 * abs(a) + 2 * abs(b) + abs(c))
            base = v_row(source, by_z[dc], 0, 1) + by_y[db] + by_x[da]
            block = [
                [stencil_ref[number * 9 + (i * 3 + j if orient == 1 else j * 3 + i)] for j in range(3)]
                for i in range(3)
            ]
            for l in range(L):
                weight = centre[l] + v_ref[pl.ds(base + 3 * 64 + l * 8, 8), :]
                wu = [weight * v_ref[pl.ds(base + j * 64 + l * 8, 8), :] for j in range(3)]
                for i in range(3):
                    term = block[i][0] * wu[0] + block[i][1] * wu[1] + block[i][2] * wu[2]
                    acc[i][l] = term if acc[i][l] is None else acc[i][l] + term
    for l in range(L):
        s = [st_ref[pl.ds(((k * 9 + a) * L + l) * 8, 8), :] for a in range(9)]
        rest = [s[i] - acc[i][l] for i in range(3)]
        inv = ((s[3], s[4], s[5]), (s[4], s[6], s[7]), (s[5], s[7], s[8]))
        for i in range(3):
            fresh[i][l] = inv[i][0] * rest[0] + inv[i][1] * rest[1] + inv[i][2] * rest[2]
            v_ref[pl.ds(v_row(cls, 0, i, l + 1), 8), :] = fresh[i][l]

    @pl.when(k < 3)
    def _():
        for i in range(3):
            fill_class(v_ref, cls, pz, i, fresh[i])


def four_colours(r, order_ref, v_ref, st_ref, stencil_ref):
    @pl.loop(0, 4)
    def _(k):
        relax(order_ref[4 * r + k], k, v_ref, st_ref, stencil_ref)


VROWS = 2 * PAD + 8 * 2 * 4 * 64
STROWS = 4 * 9 * L * 8


def prepare_kernel(xl_ref, xr_ref, own_ref, below_ref, above_ref, v_ref, st_ref, e_ref):
    v_ref[pl.ds(0, PAD), :] = jnp.zeros((PAD, 128), F32)
    v_ref[pl.ds(VROWS - PAD, PAD), :] = jnp.zeros((PAD, 128), F32)
    place_own(4, v_ref, e_ref, xl_ref, xr_ref)
    place_own_statics(0, st_ref, xl_ref, xr_ref, own_ref, below_ref, above_ref)


def first_kernel(order_ref, stencil_ref, rl_ref, rr_ref, _v, _st, v_ref, st_ref, lo_ref, hi_ref):
    place_ghosts(4, v_ref, rl_ref, rr_ref)
    place_ghost_statics(0, st_ref, rl_ref, rr_ref)
    fill_all(4, v_ref)
    four_colours(0, order_ref, v_ref, st_ref, stencil_ref)
    lowm = low(4)
    for comp in range(3):
        for p in range(4):
            for px in range(2):
                at = v_row(px * 4 + p, 0, comp, 3) + 2
                v2, v3 = v_ref[pl.ds(at, 4), :], v_ref[pl.ds(at + 8, 4), :]
                to = pl.ds((comp * 4 + p) * 8 + px, 4, stride=2)
                lo_ref[to, :] = jnp.where(lowm, v2, swap(v3))
                hi_ref[to, :] = jnp.where(lowm, swap(v2), v3)


def between_kernel(v_ref, rl_ref, xl_ref, xr_ref, rr_ref, own_ref, below_ref, above_ref, f_ref, st_ref):
    for comp in range(3):
        for l in range(L):
            for p in range(4):
                for px in range(2):
                    f_ref[pl.ds(((comp * L + l) * 4 + p) * 8 + px, 4, stride=2), :] = v_ref[
                        pl.ds(v_row(px * 4 + p, 0, comp, l + 1) + 2, 4), :
                    ]
    place_own_statics(1, st_ref, xl_ref, xr_ref, own_ref, below_ref, above_ref)
    place_ghost_statics(1, st_ref, rl_ref, rr_ref)


def prepare2_kernel(xl_ref, xr_ref, _v, v_ref, e_ref):
    place_own(3, v_ref, e_ref, xl_ref, xr_ref)


def second_kernel(order_ref, stencil_ref, rl_ref, rr_ref, st_ref, _v, out_ref, v_ref):
    place_ghosts(3, v_ref, rl_ref, rr_ref)
    fill_all(3, v_ref)
    four_colours(1, order_ref, v_ref, st_ref, stencil_ref)
    lowm = low(8)
    lane = lanes(8)
    merge = lax.shift_right_logical(lane, 1) + 64 * (lane & 1)
    for comp in range(3):
        for px in range(2):
            for py in range(2):
                cls = px * 4 + py * 2
                for l in range(L):
                    ev = v_ref[pl.ds(v_row(cls, 0, comp, l + 1), 8), :]
                    od = v_ref[pl.ds(v_row(cls + 1, 0, comp, l + 1), 8), :]
                    first = comp * 128 + px * 16 + py
                    if l >= 2:
                        out_ref[pl.ds(first + 2 * (l - 2), 4, stride=32), :] = gather(
                            jnp.where(lowm, ev, swap(od)), merge
                        )[2:6]
                    if l <= 3:
                        out_ref[pl.ds(first + 2 * (l + 4), 4, stride=32), :] = gather(
                            jnp.where(lowm, swap(ev), od), merge
                        )[2:6]


SMEM = pl.BlockSpec(memory_space=pltpu.SMEM)
VMEM = pl.BlockSpec(memory_space=pltpu.VMEM)


HBM = pl.BlockSpec(memory_space=pltpu.HBM)


def call(kernel, specs, outs, scratch, cost, aliases={}, vmem=24, extra_outs=(), extra_out_specs=(), extra_scratch=()):
    return pl.pallas_call(
        kernel,
        in_specs=specs,
        out_shape=tuple(jax.ShapeDtypeStruct((n, 128), F32) for n in outs) + tuple(extra_outs),
        out_specs=tuple(VMEM for _ in outs) + tuple(extra_out_specs),
        scratch_shapes=[pltpu.VMEM((n, 128), F32) for n in scratch] + list(extra_scratch),
        input_output_aliases=aliases,
        compiler_params=pltpu.CompilerParams(vmem_limit_bytes=vmem * 1024 * 1024),
        cost_estimate=pl.CostEstimate(flops=cost, bytes_accessed=cost, transcendentals=0),
    )


def ring(value, axis, step):
    count = lax.axis_size(axis)
    return lax.ppermute(value, axis, [(i, (i + step) % count) for i in range(count)])


def per_device(displacement, load_vector, diag_inverse, stiffness, stencil, colour):
    disp = displacement.reshape(3 * 128, 128)
    load = load_vector.reshape(3 * 128, 128)
    inv = diag_inverse.reshape(9 * 128, 128)
    stiff = stiffness.reshape(128, 128)
    colours = colour.reshape(128, 128)
    coefs = stencil.reshape(117)

    lo, hi, order, nat = call(
        pack_y_kernel,
        [HBM] * 5,
        (NF + NS, NF + NS),
        (NAT_ROWS, 8, 8),
        1 << 20,
        vmem=56,
        extra_outs=[jax.ShapeDtypeStruct((8,), jnp.int32), jax.ShapeDtypeStruct((NAT_ROWS, 128), F32)],
        extra_out_specs=[SMEM, HBM],
        extra_scratch=[pltpu.SMEM((16, 128), jnp.int32), pltpu.SemaphoreType.DMA((9,))],
    )(colours, disp, load, inv, stiff)
    above = ring(lo, "gy", -1)
    below = ring(hi, "gy", 1)
    f, s, own0, own1 = call(convert_kernel, [VMEM], (768, 864, 648, 648), (), 1 << 22)(nat)
    xl, xr = call(pack_x_kernel, [VMEM] * 4, (XF + XS, XF + XS), (), 1 << 20)(f, s, below, above)
    rr = ring(xl, "gx", -1)
    rl = ring(xr, "gx", 1)
    v, st = call(prepare_kernel, [VMEM] * 5, (VROWS, STROWS), (384,), 1 << 22)(xl, xr, own0, below, above)
    v, _, lo2, hi2 = call(
        first_kernel, [SMEM] * 2 + [VMEM] * 4, (VROWS, STROWS, 96, 96), (), 1 << 24, aliases={4: 0, 5: 1}
    )(order, coefs, rl, rr, v, st)
    above2 = ring(lo2, "gy", -1)
    below2 = ring(hi2, "gy", 1)
    f2, st = call(between_kernel, [VMEM] * 8, (576, STROWS), (), 1 << 22)(v, rl, xl, xr, rr, own1, below, above)
    xl2, xr2 = call(pack_x2_kernel, [VMEM] * 3, (288, 288), (), 1 << 20)(f2, below2, above2)
    rr2 = ring(xl2, "gx", -1)
    rl2 = ring(xr2, "gx", 1)
    (v,) = call(prepare2_kernel, [VMEM] * 3, (VROWS,), (384,), 1 << 22, aliases={2: 0})(xl2, xr2, v)
    out, _ = call(second_kernel, [SMEM] * 2 + [VMEM] * 4, (384, VROWS), (), 1 << 24, aliases={5: 1})(
        order, coefs, rl2, rr2, st, v
    )
    return out.reshape(3, XD, YD, ZD)


def solution(mesh):
    return jax.shard_map(
        per_device,
        mesh=mesh,
        in_specs=(
            P(None, "gx", "gy", None),
            P(None, "gx", "gy", None),
            P(None, None, "gx", "gy", None),
            P("gx", "gy", None),
            P(),
            P("gx", "gy", None),
        ),
        out_specs=P(None, "gx", "gy", None),
        check_vma=False,
    )
```

```python
import functools

import jax
import jax.numpy as jnp
from jax import lax
from jax.experimental import pallas as pl
from jax.experimental.pallas import tpu as pltpu
from jax.sharding import PartitionSpec as P

XD, YD, ZD = 8, 16, 128
L = 6
PAD = 8
F32 = jnp.float32

offsets = [
    (a, b, c)
    for a in (-1, 0, 1)
    for b in (-1, 0, 1)
    for c in (-1, 0, 1)
    if (a, b, c) > (0, 0, 0)
]

NF = 16 * 8
NS = 18 * 8
XF = 4 * L * 4 * 4
XS = 18 * L * 4


def lanes(rows):
    return lax.broadcasted_iota(jnp.int32, (rows, 128), 1)


def low(rows):
    return lanes(rows) < 64


def gather(v, idx):
    return jnp.take_along_axis(v, idx, axis=1, mode="promise_in_bounds")


def split_idx(rows, first):
    lane = lanes(rows)
    return jnp.where(lane < 64, 2 * lane + first, 2 * lane - 127 - first)


def swap(v):
    return pltpu.roll(v, 64, 1)


def parity(cls):
    return lax.shift_right_logical(cls, 2), lax.shift_right_logical(cls, 1) & 1, cls & 1


def load_rows(nat, first, cls_row, y1, count):
    return nat[pl.ds(first + cls_row + 2 * y1, count, stride=32), :]


NAT_LOAD, NAT_INV, NAT_STIFF, NAT_ORDER, NAT_ROWS = 384, 768, 1536, 1664, 1672


def static_rows():
    return [NAT_LOAD + i * 128 for i in range(3)] + [NAT_INV + i * 128 for i in range(6)]


def field_rows():
    return [0, 128, 256, NAT_STIFF]


def pack_y_kernel(
    colour_hbm, disp_hbm, load_hbm, inv_hbm, stiff_hbm,
    lo_ref, hi_ref, order_ref, nat_hbm, nat_ref, colour_s, sems,
):
    moves = [
        (colour_hbm.at[pl.ds(0, 8)], colour_s.at[pl.ds(0, 8)]),
        (colour_hbm.at[pl.ds(16, 8)], colour_s.at[pl.ds(8, 8)]),
        (disp_hbm, nat_ref.at[pl.ds(0, 384)]),
        (stiff_hbm, nat_ref.at[pl.ds(NAT_STIFF, 128)]),
        (load_hbm, nat_ref.at[pl.ds(NAT_LOAD, 384)]),
        (inv_hbm.at[pl.ds(0, 384)], nat_ref.at[pl.ds(NAT_INV, 384)]),
        (inv_hbm.at[pl.ds(512, 256)], nat_ref.at[pl.ds(NAT_INV + 384, 256)]),
        (inv_hbm.at[pl.ds(1024, 128)], nat_ref.at[pl.ds(NAT_INV + 640, 128)]),
    ]
    copies = [pltpu.make_async_copy(a, b, sems.at[i]) for i, (a, b) in enumerate(moves)]
    for copy in copies:
        copy.start()

    def keep(first, count, i):
        part = pl.ds(first, count)
        copy = pltpu.make_async_copy(nat_ref.at[part], nat_hbm.at[part], sems.at[8 + i])
        copy.start()
        return copy

    copies[0].wait()
    copies[1].wait()
    for cls in range(8):
        px, py, pz = cls >> 2, (cls >> 1) & 1, cls & 1
        order_ref[colour_s[8 * px + py, pz]] = cls
    for k in range(8):
        nat_ref[pl.ds(NAT_ORDER + k, 1), :] = jnp.full((1, 128), order_ref[k].astype(F32))
    copies[2].wait()
    copies[3].wait()
    kept = [keep(0, 384, 0), keep(NAT_STIFF, 136, 1)]
    lowm = low(8)
    idx_e = split_idx(8, 0)
    for comp, first in enumerate(field_rows()):
        for py in range(2):
            for out, y1 in ((lo_ref, 0), (hi_ref, 6)):
                a = nat_ref[pl.ds(first + py + 2 * y1, 8, stride=16), :]
                b = nat_ref[pl.ds(first + py + 2 * y1 + 2, 8, stride=16), :]
                if comp == 3:
                    a, b = 0.5 * a, 0.5 * b
                a, b = gather(a, idx_e), gather(b, idx_e)
                row = (comp * 4 + py * 2) * 8
                out[pl.ds(row, 8), :] = jnp.where(lowm, a, swap(b))
                out[pl.ds(row + 8, 8), :] = jnp.where(lowm, swap(a), b)
    for copy in copies[4:]:
        copy.wait()
    kept.append(keep(NAT_LOAD, 1152, 2))
    sub = lax.broadcasted_iota(jnp.int32, (8, 128), 0)
    second, third, upper = (sub & 3) == 2, (sub & 3) == 3, sub >= 4

    def rows(start, stride):
        return nat_ref[pl.ds(start, 8, stride=stride), :]

    for r in range(2):
        px, py, pz = zip(*[parity(order_ref[4 * r + k]) for k in range(3)])
        cls_row = [px[k] * 16 + py[k] for k in range(3)]
        idx = 2 * (lanes(8) & 63) + jnp.where(second, pz[1], jnp.where(third, pz[2], pz[0]))
        for side, out in ((0, lo_ref), (1, hi_ref)):
            near, far = (0, 1) if side == 0 else (7, 6)
            for a, first in enumerate(static_rows()):
                at = [first + 2 * near + cls_row[k] for k in range(3)]
                at_far = first + 2 * far + cls_row[0]
                nv = jnp.where(upper, rows(at[0] - 64, 32), rows(at[0], 32))
                nv = jnp.where(second, rows(at[1] - 48, 24), jnp.where(third, rows(at[2] - 72, 24), nv))
                fv = jnp.where(upper, rows(at_far - 64, 32), rows(at_far, 32))
                fv = jnp.where(second, rows(at[1] + 16, 8), jnp.where(third, rows(at[2] + 8, 8), fv))
                nv, fv = gather(nv, idx), gather(fv, idx)
                out[pl.ds(NF + (r * 9 + a) * 8, 8), :] = (
                    jnp.where(lowm, nv, fv) if side == 0 else jnp.where(lowm, fv, nv)
                )
    for copy in kept:
        copy.wait()


def convert_kernel(nat_ref, f_ref, s_ref, own0_ref, own1_ref):
    lowm = low(8)
    low4 = low(4)
    idx_e = split_idx(8, 0)
    zero = jnp.zeros((8, 128), F32)
    for comp, first in enumerate(field_rows()):
        for py in range(2):
            ev, od = [], []
            for y1 in range(8):
                v = nat_ref[pl.ds(first + py + 2 * y1, 8, stride=16), :]
                if comp == 3:
                    v = 0.5 * v
                v = gather(v, idx_e)
                ev.append(v)
                od.append(swap(v))
            for l in range(L):
                e0, o0 = (ev[l - 2], od[l - 2]) if l >= 2 else (zero, zero)
                e1, o1 = (ev[l + 4], od[l + 4]) if l <= 3 else (zero, zero)
                row = ((comp * L + l) * 4 + py * 2) * 8
                f_ref[pl.ds(row, 8), :] = jnp.where(lowm, e0, o1)
                f_ref[pl.ds(row + 8, 8), :] = jnp.where(lowm, o0, e1)
    zero4 = jnp.zeros((4, 128), F32)
    for r, own in ((0, own0_ref), (1, own1_ref)):
        for k in range(4):
            px, py, pz = parity(nat_ref[NAT_ORDER + 4 * r + k, 0].astype(jnp.int32))
            cls_row = px * 16 + py
            idx0, idx1 = split_idx(4, pz), split_idx(4, 1 - pz)
            for a, first in enumerate(static_rows()):
                rows = [load_rows(nat_ref, first, cls_row, y1, 4) for y1 in range(8)]
                for l in range(L):
                    v0 = gather(rows[l - 2], idx0) if l >= 2 else zero4
                    v1 = gather(rows[l + 4], idx1) if l <= 3 else zero4
                    v = jnp.where(low4, v0, v1)
                    srow = ((r * 9 + a) * L + l) * 8
                    if k == 0:
                        s_ref[pl.ds(srow, 2), :] = v[0:2]
                        s_ref[pl.ds(srow + 4, 2), :] = v[2:4]
                    else:
                        own[pl.ds((((k - 1) * 9 + a) * L + l) * 4, 4), :] = v
                        if k < 3:
                            s_ref[pl.ds(srow + 1 + k, 1), :] = v[0:1]
                            s_ref[pl.ds(srow + 5 + k, 1), :] = v[3:4]


def add_y(v, l, below, above, lowm):
    if l == 0:
        return jnp.where(lowm, below, v)
    if l == 1:
        return jnp.where(lowm, swap(below), v)
    if l == 4:
        return jnp.where(lowm, v, swap(above))
    if l == 5:
        return jnp.where(lowm, v, above)
    return v


def put_pair(xl_ref, xr_ref, row, v, w):
    sub = lax.broadcasted_iota(jnp.int32, (8, 128), 0) < 4
    xl_ref[pl.ds(row, 8), :] = jnp.where(sub, v, pltpu.roll(w, 4, 0))
    xr_ref[pl.ds(row, 8), :] = jnp.where(sub, pltpu.roll(v, 4, 0), w)


def by_side(one, two, run):
    even = lax.axis_index("gx") % 2 == 0

    @pl.when(even)
    def _():
        run(two, one)

    @pl.when(jnp.logical_not(even))
    def _():
        run(one, two)


def y_masks():
    gy = lax.axis_index("gy")
    return (
        jnp.where(gy > 0, 1.0, 0.0).astype(F32),
        jnp.where(gy < lax.axis_size("gy") - 1, 1.0, 0.0).astype(F32),
    )


def x_masks():
    gx = lax.axis_index("gx")
    return (
        jnp.where(gx > 0, 1.0, 0.0).astype(F32),
        jnp.where(gx < lax.axis_size("gx") - 1, 1.0, 0.0).astype(F32),
    )


def pack_x_fields(comps, f_ref, below_ref, above_ref, xl_ref, xr_ref):
    lowm = low(8)
    m_below, m_above = y_masks()
    for comp in range(comps):
        for half in range(2):
            below = [below_ref[pl.ds((comp * 4 + 2 * half + i) * 8, 8), :] * m_below for i in range(2)]
            above = [above_ref[pl.ds((comp * 4 + 2 * half + i) * 8, 8), :] * m_above for i in range(2)]
            for l in range(L):
                row = (comp * L + l) * 4 + 2 * half
                v = [add_y(f_ref[pl.ds((row + i) * 8, 8), :], l, below[i], above[i], lowm) for i in range(2)]
                put_pair(xl_ref, xr_ref, row * 4, v[0], v[1])


def pack_x_kernel(f_ref, s_ref, below_ref, above_ref, one_ref, two_ref):
    by_side(one_ref, two_ref, functools.partial(pack_x, f_ref, s_ref, below_ref, above_ref))


def pack_x(f_ref, s_ref, below_ref, above_ref, xl_ref, xr_ref):
    pack_x_fields(4, f_ref, below_ref, above_ref, xl_ref, xr_ref)
    lowm = low(8)
    m_below, m_above = y_masks()
    for ra in range(18):
        below = below_ref[pl.ds(NF + ra * 8, 8), :] * m_below
        above = above_ref[pl.ds(NF + ra * 8, 8), :] * m_above
        for l in range(0, L, 2):
            row = ra * L + l
            v = [add_y(s_ref[pl.ds((row + i) * 8, 8), :], l + i, below, above, lowm) for i in range(2)]
            put_pair(xl_ref, xr_ref, XF + row * 4, v[0], v[1])


def pack_x2_kernel(f_ref, below_ref, above_ref, one_ref, two_ref):
    by_side(one_ref, two_ref, functools.partial(pack_x_fields, 3, f_ref, below_ref, above_ref))


def v_row(cls, shifted, comp, ext):
    return PAD + (((cls * 2 + shifted) * 4 + comp) * 8 + ext) * 8


def fill_class(v_ref, cls, pz, comp, v):
    low_edge = pz == 1
    if isinstance(pz, int):
        shift, edge = (1, 0) if low_edge else (127, 63)
        shift_swap = (shift + 64) % 128
    else:
        shift, edge = jnp.where(low_edge, 1, 127), jnp.where(low_edge, 0, 63)
        shift_swap = jnp.where(low_edge, 65, 63)
    keep = (lanes(8) & 63) != edge
    base = v_row(cls, 0, comp, 0)
    moved = v_row(cls, 1, comp, 0)
    for l in (0, L - 1):
        ext = 56 if l == 0 else 0
        v_ref[pl.ds(base + ext, 8), :] = swap(v[l])
        v_ref[pl.ds(moved + ext, 8), :] = jnp.where(keep, pltpu.roll(v[l], shift_swap, 1), 0.0)
    for l in range(L):
        v_ref[pl.ds(moved + (l + 1) * 8, 8), :] = jnp.where(keep, pltpu.roll(v[l], shift, 1), 0.0)


def fill_all(comps, v_ref):
    for comp in range(comps):
        for cls in range(8):
            base = v_row(cls, 0, comp, 1)
            fill_class(v_ref, cls, cls & 1, comp, [v_ref[pl.ds(base + l * 8, 8), :] for l in range(L)])


def place_own(comps, v_ref, e_ref, xl_ref, xr_ref):
    zero = jnp.zeros((8, 128), F32)
    sub = lax.broadcasted_iota(jnp.int32, (8, 128), 0) < 4
    for comp in range(comps):
        for l in range(L):
            for p in (0, 2):
                row = ((comp * L + l) * 4 + p) * 4
                a, b = xl_ref[pl.ds(row, 8), :], xr_ref[pl.ds(row, 8), :]
                at = (l * 4 + p) * 16
                e_ref[pl.ds(at + 4, 8), :] = jnp.where(sub, a, pltpu.roll(b, 4, 0))
                e_ref[pl.ds(at + 20, 8), :] = jnp.where(sub, pltpu.roll(a, 4, 0), b)
        for l in range(L):
            for p in range(4):
                for px in range(2):
                    v_ref[pl.ds(v_row(px * 4 + p, 0, comp, l + 1), 8), :] = e_ref[
                        pl.ds((l * 4 + p) * 16 + px, 8, stride=2), :
                    ]


def place_ghosts(comps, v_ref, rl_ref, rr_ref):
    m_left, m_right = x_masks()
    for comp in range(comps):
        for p in range(4):
            for px in range(2):
                base = v_row(px * 4 + p, 0, comp, 1)
                for i in range(2):
                    row = (comp * L * 4 + p) * 4 + px + 2 * i
                    v_ref[pl.ds(base + i, L, stride=8), :] = rl_ref[pl.ds(row, L, stride=16), :] * m_left
                    v_ref[pl.ds(base + 6 + i, L, stride=8), :] = rr_ref[pl.ds(row, L, stride=16), :] * m_right


def place_own_statics(r, st_ref, xl_ref, xr_ref, own_ref, below_ref, above_ref):
    m_below, m_above = y_masks()
    lowm = low(1)
    zero = jnp.zeros((8, 128), F32)
    for a in range(9):
        below = below_ref[pl.ds(NF + (r * 9 + a) * 8, 8), :] * m_below
        above = above_ref[pl.ds(NF + (r * 9 + a) * 8, 8), :] * m_above
        for l in range(L):
            srow = XF + ((r * 9 + a) * L + l) * 4
            own_l, own_r = xl_ref[pl.ds(srow, 4), :], xr_ref[pl.ds(srow, 4), :]
            at = (a * L + l) * 8
            st_ref[pl.ds(at, 8), :] = zero
            st_ref[pl.ds(at + 2, 2), :] = own_l[0:2]
            st_ref[pl.ds(at + 4, 2), :] = own_r[0:2]
            for k in (1, 2, 3):
                at = ((k * 9 + a) * L + l) * 8
                st_ref[pl.ds(at, 8), :] = zero
                st_ref[pl.ds(at + 2, 4), :] = own_ref[pl.ds((((k - 1) * 9 + a) * L + l) * 4, 4), :]
                if k < 3:
                    st_ref[pl.ds(at + 2, 1), :] = own_l[1 + k : 2 + k]
                    st_ref[pl.ds(at + 5, 1), :] = own_r[1 + k : 2 + k]
                    for q in range(2):
                        at_q = at + 3 + q
                        if l == 1:
                            st_ref[pl.ds(at_q, 1), :] = jnp.where(
                                lowm, below[1 + k + 4 * q : 2 + k + 4 * q], st_ref[pl.ds(at_q, 1), :]
                            )
                        if l == 4:
                            st_ref[pl.ds(at_q, 1), :] = jnp.where(
                                lowm, st_ref[pl.ds(at_q, 1), :], above[1 + k + 4 * q : 2 + k + 4 * q]
                            )


def place_ghost_statics(r, st_ref, rl_ref, rr_ref):
    m_left, m_right = x_masks()
    for a in range(9):
        for row, k, at_l, at_r in ((0, 0, 0, 6), (1, 0, 1, 7), (2, 1, 1, 6), (3, 2, 1, 6)):
            src = pl.ds(XF + (r * 9 + a) * L * 4 + row, L, stride=4)
            base = (k * 9 + a) * L * 8
            st_ref[pl.ds(base + at_l, L, stride=8), :] = rl_ref[src, :] * m_left
            st_ref[pl.ds(base + at_r, L, stride=8), :] = rr_ref[src, :] * m_right


def relax(cls, k, v_ref, st_ref, stencil_ref):
    px, py, pz = parity(cls)
    by_x = {0: 0, -1: px - 1, 1: px}
    by_y = {0: 0, -1: (py - 1) * 8, 1: py * 8}
    by_z = {0: 0, -1: 1 - pz, 1: pz}
    centre = [v_ref[pl.ds(v_row(cls, 0, 3, l + 1), 8), :] for l in range(L)]
    acc = [[None] * L for _ in range(3)]
    fresh = [[None] * L for _ in range(3)]
    for number, (a, b, c) in enumerate(offsets):
        for orient in (1, -1):
            da, db, dc = orient * a, orient * b, orient * c
            source = cls ^ (4 * abs(a) + 2 * abs(b) + abs(c))
            base = v_row(source, by_z[dc], 0, 1) + by_y[db] + by_x[da]
            block = [
                [stencil_ref[number * 9 + (i * 3 + j if orient == 1 else j * 3 + i)] for j in range(3)]
                for i in range(3)
            ]
            for l in range(L):
                weight = centre[l] + v_ref[pl.ds(base + 3 * 64 + l * 8, 8), :]
                wu = [weight * v_ref[pl.ds(base + j * 64 + l * 8, 8), :] for j in range(3)]
                for i in range(3):
                    term = block[i][0] * wu[0] + block[i][1] * wu[1] + block[i][2] * wu[2]
                    acc[i][l] = term if acc[i][l] is None else acc[i][l] + term
    for l in range(L):
        s = [st_ref[pl.ds(((k * 9 + a) * L + l) * 8, 8), :] for a in range(9)]
        rest = [s[i] - acc[i][l] for i in range(3)]
        inv = ((s[3], s[4], s[5]), (s[4], s[6], s[7]), (s[5], s[7], s[8]))
        for i in range(3):
            fresh[i][l] = inv[i][0] * rest[0] + inv[i][1] * rest[1] + inv[i][2] * rest[2]
            v_ref[pl.ds(v_row(cls, 0, i, l + 1), 8), :] = fresh[i][l]

    @pl.when(k < 3)
    def _():
        for i in range(3):
            fill_class(v_ref, cls, pz, i, fresh[i])


def four_colours(r, order_ref, v_ref, st_ref, stencil_ref):
    @pl.loop(0, 4)
    def _(k):
        relax(order_ref[4 * r + k], k, v_ref, st_ref, stencil_ref)


VROWS = 2 * PAD + 8 * 2 * 4 * 64
STROWS = 4 * 9 * L * 8


def prepare_kernel(one_ref, two_ref, own_ref, below_ref, above_ref, v_ref, st_ref, e_ref):
    v_ref[pl.ds(0, PAD), :] = jnp.zeros((PAD, 128), F32)
    v_ref[pl.ds(VROWS - PAD, PAD), :] = jnp.zeros((PAD, 128), F32)

    def place(xl_ref, xr_ref):
        place_own(4, v_ref, e_ref, xl_ref, xr_ref)
        place_own_statics(0, st_ref, xl_ref, xr_ref, own_ref, below_ref, above_ref)

    by_side(one_ref, two_ref, place)


def first_kernel(order_ref, stencil_ref, one_ref, two_ref, _v, _st, v_ref, st_ref, lo_ref, hi_ref):

    def place(rl_ref, rr_ref):
        place_ghosts(4, v_ref, rl_ref, rr_ref)
        place_ghost_statics(0, st_ref, rl_ref, rr_ref)

    by_side(one_ref, two_ref, place)
    fill_all(4, v_ref)
    four_colours(0, order_ref, v_ref, st_ref, stencil_ref)
    lowm = low(4)
    for comp in range(3):
        for p in range(4):
            for px in range(2):
                at = v_row(px * 4 + p, 0, comp, 3) + 2
                v2, v3 = v_ref[pl.ds(at, 4), :], v_ref[pl.ds(at + 8, 4), :]
                to = pl.ds((comp * 4 + p) * 8 + px, 4, stride=2)
                lo_ref[to, :] = jnp.where(lowm, v2, swap(v3))
                hi_ref[to, :] = jnp.where(lowm, swap(v2), v3)


def between_kernel(v_ref, r1_ref, x1_ref, x2_ref, r2_ref, own_ref, below_ref, above_ref, f_ref, st_ref):
    for comp in range(3):
        for l in range(L):
            for p in range(4):
                for px in range(2):
                    f_ref[pl.ds(((comp * L + l) * 4 + p) * 8 + px, 4, stride=2), :] = v_ref[
                        pl.ds(v_row(px * 4 + p, 0, comp, l + 1) + 2, 4), :
                    ]

    def place(left, right):
        place_own_statics(1, st_ref, left[0], right[0], own_ref, below_ref, above_ref)
        place_ghost_statics(1, st_ref, left[1], right[1])

    by_side((x1_ref, r1_ref), (x2_ref, r2_ref), place)


def prepare2_kernel(one_ref, two_ref, _v, v_ref, e_ref):
    by_side(one_ref, two_ref, functools.partial(place_own, 3, v_ref, e_ref))


def second_kernel(order_ref, stencil_ref, one_ref, two_ref, st_ref, _v, v_ref, out_ref):
    by_side(one_ref, two_ref, functools.partial(place_ghosts, 3, v_ref))
    fill_all(3, v_ref)
    four_colours(1, order_ref, v_ref, st_ref, stencil_ref)
    lowm = low(8)
    lane = lanes(8)
    merge = lax.shift_right_logical(lane, 1) + 64 * (lane & 1)
    for comp in range(3):
        for px in range(2):
            for py in range(2):
                cls = px * 4 + py * 2
                for l in range(L):
                    ev = v_ref[pl.ds(v_row(cls, 0, comp, l + 1), 8), :]
                    od = v_ref[pl.ds(v_row(cls + 1, 0, comp, l + 1), 8), :]
                    first = comp * 128 + px * 16 + py
                    if l >= 2:
                        out_ref[pl.ds(first + 2 * (l - 2), 4, stride=32), :] = gather(
                            jnp.where(lowm, ev, swap(od)), merge
                        )[2:6]
                    if l <= 3:
                        out_ref[pl.ds(first + 2 * (l + 4), 4, stride=32), :] = gather(
                            jnp.where(lowm, swap(ev), od), merge
                        )[2:6]


SMEM = pl.BlockSpec(memory_space=pltpu.SMEM)
VMEM = pl.BlockSpec(memory_space=pltpu.VMEM)


HBM = pl.BlockSpec(memory_space=pltpu.HBM)


def call(kernel, specs, outs, scratch, cost, aliases={}, vmem=24, extra_outs=(), extra_out_specs=(), extra_scratch=()):
    return pl.pallas_call(
        kernel,
        in_specs=specs,
        out_shape=tuple(jax.ShapeDtypeStruct((n, 128), F32) for n in outs) + tuple(extra_outs),
        out_specs=tuple(VMEM for _ in outs) + tuple(extra_out_specs),
        scratch_shapes=[pltpu.VMEM((n, 128), F32) for n in scratch] + list(extra_scratch),
        input_output_aliases=aliases,
        compiler_params=pltpu.CompilerParams(vmem_limit_bytes=vmem * 1024 * 1024),
        cost_estimate=pl.CostEstimate(flops=cost, bytes_accessed=cost, transcendentals=0),
    )


def ring(value, axis, step):
    count = lax.axis_size(axis)
    return lax.ppermute(value, axis, [(i, (i + step) % count) for i in range(count)])


def swaps(one, two):
    n = lax.axis_size("gx")
    first = [(i, i ^ 1) for i in range(n)]
    second = [(i, (i + 1 if i % 2 else i - 1) % n) for i in range(n)]
    far = lax.ppermute(two, "gx", second)
    return lax.ppermute(one, "gx", first), far


def per_device(displacement, load_vector, diag_inverse, stiffness, stencil, colour):
    disp = displacement.reshape(3 * 128, 128)
    load = load_vector.reshape(3 * 128, 128)
    inv = diag_inverse.reshape(9 * 128, 128)
    stiff = stiffness.reshape(128, 128)
    colours = colour.reshape(128, 128)
    coefs = stencil.reshape(117)

    lo, hi, order, nat = call(
        pack_y_kernel,
        [HBM] * 5,
        (NF + NS, NF + NS),
        (NAT_ROWS,),
        1 << 20,
        vmem=56,
        extra_outs=[jax.ShapeDtypeStruct((8,), jnp.int32), jax.ShapeDtypeStruct((NAT_ROWS, 128), F32)],
        extra_out_specs=[SMEM, HBM],
        extra_scratch=[pltpu.SMEM((16, 128), jnp.int32), pltpu.SemaphoreType.DMA((11,))],
    )(colours, disp, load, inv, stiff)
    above = ring(lo, "gy", -1)
    below = ring(hi, "gy", 1)
    f, s, own0, own1 = call(convert_kernel, [VMEM], (768, 864, 648, 648), (), 1 << 22)(nat)
    x1, x2 = call(pack_x_kernel, [VMEM] * 4, (XF + XS, XF + XS), (), 1 << 20)(f, s, below, above)
    r1, r2 = swaps(x1, x2)
    v, st = call(prepare_kernel, [VMEM] * 5, (VROWS, STROWS), (384,), 1 << 22)(x1, x2, own0, below, above)
    v, _, lo2, hi2 = call(
        first_kernel, [SMEM] * 2 + [VMEM] * 4, (VROWS, STROWS, 96, 96), (), 1 << 24, aliases={4: 0, 5: 1}
    )(order, coefs, r1, r2, v, st)
    above2 = ring(lo2, "gy", -1)
    below2 = ring(hi2, "gy", 1)
    f2, st = call(between_kernel, [VMEM] * 8, (576, STROWS), (), 1 << 22)(v, r1, x1, x2, r2, own1, below, above)
    x1, x2 = call(pack_x2_kernel, [VMEM] * 3, (288, 288), (), 1 << 20)(f2, below2, above2)
    r1, r2 = swaps(x1, x2)
    (v,) = call(prepare2_kernel, [VMEM] * 3, (VROWS,), (384,), 1 << 22, aliases={2: 0})(x1, x2, v)
    v, out = call(second_kernel, [SMEM] * 2 + [VMEM] * 4, (VROWS, 384), (), 1 << 24, aliases={5: 0})(
        order, coefs, r1, r2, st, v
    )
    return out.reshape(3, XD, YD, ZD)


def solution(mesh):
    return jax.shard_map(
        per_device,
        mesh=mesh,
        in_specs=(
            P(None, "gx", "gy", None),
            P(None, "gx", "gy", None),
            P(None, None, "gx", "gy", None),
            P("gx", "gy", None),
            P(),
            P("gx", "gy", None),
        ),
        out_specs=P(None, "gx", "gy", None),
        check_vma=False,
    )
```

```python
import functools

import jax
import jax.numpy as jnp
from jax import lax
from jax.experimental import pallas as pl
from jax.experimental.pallas import tpu as pltpu
from jax.sharding import PartitionSpec as P

XD, YD, ZD = 8, 16, 128
L = 6
PAD = 8
F32 = jnp.float32

offsets = [
    (a, b, c)
    for a in (-1, 0, 1)
    for b in (-1, 0, 1)
    for c in (-1, 0, 1)
    if (a, b, c) > (0, 0, 0)
]

NF = 16 * 8
NS = 18 * 8
XF = 4 * L * 4 * 4
XS = 9 * L * 4


def lanes(rows):
    return lax.broadcasted_iota(jnp.int32, (rows, 128), 1)


def low(rows):
    return lanes(rows) < 64


def gather(v, idx):
    return jnp.take_along_axis(v, idx, axis=1, mode="promise_in_bounds")


def split_idx(rows, first):
    lane = lanes(rows)
    return jnp.where(lane < 64, 2 * lane + first, 2 * lane - 127 - first)


def swap(v):
    return pltpu.roll(v, 64, 1)


def parity(cls):
    return lax.shift_right_logical(cls, 2), lax.shift_right_logical(cls, 1) & 1, cls & 1


def load_rows(nat, first, cls_row, y1, count):
    return nat[pl.ds(first + cls_row + 2 * y1, count, stride=32), :]


NAT_LOAD, NAT_INV, NAT_STIFF, NAT_ORDER, NAT_ROWS = 384, 768, 1536, 1664, 1672


def static_rows():
    return [NAT_LOAD + i * 128 for i in range(3)] + [NAT_INV + i * 128 for i in range(6)]


def field_rows():
    return [0, 128, 256, NAT_STIFF]


def pack_y_kernel(
    colour_hbm, disp_hbm, load_hbm, inv_hbm, stiff_hbm,
    lo_ref, hi_ref, order_ref, nat_hbm, nat_ref, colour_s, sems,
):
    moves = [
        (colour_hbm.at[pl.ds(0, 8)], colour_s.at[pl.ds(0, 8)]),
        (colour_hbm.at[pl.ds(16, 8)], colour_s.at[pl.ds(8, 8)]),
        (disp_hbm, nat_ref.at[pl.ds(0, 384)]),
        (stiff_hbm, nat_ref.at[pl.ds(NAT_STIFF, 128)]),
        (load_hbm, nat_ref.at[pl.ds(NAT_LOAD, 384)]),
        (inv_hbm.at[pl.ds(0, 384)], nat_ref.at[pl.ds(NAT_INV, 384)]),
        (inv_hbm.at[pl.ds(512, 256)], nat_ref.at[pl.ds(NAT_INV + 384, 256)]),
        (inv_hbm.at[pl.ds(1024, 128)], nat_ref.at[pl.ds(NAT_INV + 640, 128)]),
    ]
    copies = [pltpu.make_async_copy(a, b, sems.at[i]) for i, (a, b) in enumerate(moves)]
    for copy in copies:
        copy.start()

    def keep(first, count, i):
        part = pl.ds(first, count)
        copy = pltpu.make_async_copy(nat_ref.at[part], nat_hbm.at[part], sems.at[8 + i])
        copy.start()
        return copy

    copies[2].wait()
    copies[3].wait()
    kept = [keep(0, 384, 0), keep(NAT_STIFF, 128, 1)]
    lowm = low(8)
    idx_e = split_idx(8, 0)
    for comp, first in enumerate(field_rows()):
        for py in range(2):
            for out, y1 in ((lo_ref, 0), (hi_ref, 6)):
                a = nat_ref[pl.ds(first + py + 2 * y1, 8, stride=16), :]
                b = nat_ref[pl.ds(first + py + 2 * y1 + 2, 8, stride=16), :]
                if comp == 3:
                    a, b = 0.5 * a, 0.5 * b
                a, b = gather(a, idx_e), gather(b, idx_e)
                row = (comp * 4 + py * 2) * 8
                out[pl.ds(row, 8), :] = jnp.where(lowm, a, swap(b))
                out[pl.ds(row + 8, 8), :] = jnp.where(lowm, swap(a), b)
    copies[0].wait()
    copies[1].wait()
    for cls in range(8):
        px, py, pz = cls >> 2, (cls >> 1) & 1, cls & 1
        order_ref[colour_s[8 * px + py, pz]] = cls
    for k in range(8):
        nat_ref[pl.ds(NAT_ORDER + k, 1), :] = jnp.full((1, 128), order_ref[k].astype(F32))
    kept.append(keep(NAT_ORDER, 8, 3))
    for copy in copies[4:]:
        copy.wait()
    kept.append(keep(NAT_LOAD, 1152, 2))
    sub = lax.broadcasted_iota(jnp.int32, (8, 128), 0)
    second, third, upper = (sub & 3) == 2, (sub & 3) == 3, sub >= 4

    def rows(start, stride):
        return nat_ref[pl.ds(start, 8, stride=stride), :]

    for r in range(2):
        px, py, pz = zip(*[parity(order_ref[4 * r + k]) for k in range(3)])
        cls_row = [px[k] * 16 + py[k] for k in range(3)]
        idx = 2 * (lanes(8) & 63) + jnp.where(second, pz[1], jnp.where(third, pz[2], pz[0]))
        for side, out in ((0, lo_ref), (1, hi_ref)):
            near, far = (0, 1) if side == 0 else (7, 6)
            for a, first in enumerate(static_rows()):
                at = [first + 2 * near + cls_row[k] for k in range(3)]
                at_far = first + 2 * far + cls_row[0]
                nv = jnp.where(upper, rows(at[0] - 64, 32), rows(at[0], 32))
                nv = jnp.where(second, rows(at[1] - 48, 24), jnp.where(third, rows(at[2] - 72, 24), nv))
                fv = jnp.where(upper, rows(at_far - 64, 32), rows(at_far, 32))
                fv = jnp.where(second, rows(at[1] + 16, 8), jnp.where(third, rows(at[2] + 8, 8), fv))
                nv, fv = gather(nv, idx), gather(fv, idx)
                out[pl.ds(NF + (r * 9 + a) * 8, 8), :] = (
                    jnp.where(lowm, nv, fv) if side == 0 else jnp.where(lowm, fv, nv)
                )
    for copy in kept:
        copy.wait()


def convert_kernel(nat_ref, f_ref, s_ref, own0_ref, own1_ref):
    lowm = low(8)
    low4 = low(4)
    idx_e = split_idx(8, 0)
    zero = jnp.zeros((8, 128), F32)
    for comp, first in enumerate(field_rows()):
        for py in range(2):
            ev, od = [], []
            for y1 in range(8):
                v = nat_ref[pl.ds(first + py + 2 * y1, 8, stride=16), :]
                if comp == 3:
                    v = 0.5 * v
                v = gather(v, idx_e)
                ev.append(v)
                od.append(swap(v))
            for l in range(L):
                e0, o0 = (ev[l - 2], od[l - 2]) if l >= 2 else (zero, zero)
                e1, o1 = (ev[l + 4], od[l + 4]) if l <= 3 else (zero, zero)
                row = ((comp * L + l) * 4 + py * 2) * 8
                f_ref[pl.ds(row, 8), :] = jnp.where(lowm, e0, o1)
                f_ref[pl.ds(row + 8, 8), :] = jnp.where(lowm, o0, e1)
    zero4 = jnp.zeros((4, 128), F32)
    for r, own in ((0, own0_ref), (1, own1_ref)):
        for k in range(4):
            px, py, pz = parity(nat_ref[NAT_ORDER + 4 * r + k, 0].astype(jnp.int32))
            cls_row = px * 16 + py
            idx0, idx1 = split_idx(4, pz), split_idx(4, 1 - pz)
            for a, first in enumerate(static_rows()):
                rows = [load_rows(nat_ref, first, cls_row, y1, 4) for y1 in range(8)]
                for l in range(L):
                    v0 = gather(rows[l - 2], idx0) if l >= 2 else zero4
                    v1 = gather(rows[l + 4], idx1) if l <= 3 else zero4
                    v = jnp.where(low4, v0, v1)
                    srow = ((r * 9 + a) * L + l) * 8
                    if k == 0:
                        s_ref[pl.ds(srow, 2), :] = v[0:2]
                        s_ref[pl.ds(srow + 4, 2), :] = v[2:4]
                    else:
                        own[pl.ds((((k - 1) * 9 + a) * L + l) * 4, 4), :] = v
                        if k < 3:
                            s_ref[pl.ds(srow + 1 + k, 1), :] = v[0:1]
                            s_ref[pl.ds(srow + 5 + k, 1), :] = v[3:4]


def add_y(v, l, below, above, lowm):
    if l == 0:
        return jnp.where(lowm, below, v)
    if l == 1:
        return jnp.where(lowm, swap(below), v)
    if l == 4:
        return jnp.where(lowm, v, swap(above))
    if l == 5:
        return jnp.where(lowm, v, above)
    return v


def put_pair(xl_ref, xr_ref, row, v, w):
    sub = lax.broadcasted_iota(jnp.int32, (8, 128), 0) < 4
    xl_ref[pl.ds(row, 8), :] = jnp.where(sub, v, pltpu.roll(w, 4, 0))
    xr_ref[pl.ds(row, 8), :] = jnp.where(sub, pltpu.roll(v, 4, 0), w)


def by_side(one, two, run):
    even = lax.axis_index("gx") % 2 == 0

    @pl.when(even)
    def _():
        run(two, one)

    @pl.when(jnp.logical_not(even))
    def _():
        run(one, two)


def y_masks():
    gy = lax.axis_index("gy")
    return (
        jnp.where(gy > 0, 1.0, 0.0).astype(F32),
        jnp.where(gy < lax.axis_size("gy") - 1, 1.0, 0.0).astype(F32),
    )


def x_masks():
    gx = lax.axis_index("gx")
    return (
        jnp.where(gx > 0, 1.0, 0.0).astype(F32),
        jnp.where(gx < lax.axis_size("gx") - 1, 1.0, 0.0).astype(F32),
    )


def pack_x_fields(comps, f_ref, below_ref, above_ref, xl_ref, xr_ref):
    lowm = low(8)
    m_below, m_above = y_masks()
    for comp in range(comps):
        for half in range(2):
            below = [below_ref[pl.ds((comp * 4 + 2 * half + i) * 8, 8), :] * m_below for i in range(2)]
            above = [above_ref[pl.ds((comp * 4 + 2 * half + i) * 8, 8), :] * m_above for i in range(2)]
            for l in range(L):
                row = (comp * L + l) * 4 + 2 * half
                v = [add_y(f_ref[pl.ds((row + i) * 8, 8), :], l, below[i], above[i], lowm) for i in range(2)]
                put_pair(xl_ref, xr_ref, row * 4, v[0], v[1])


def pack_x_kernel(f_ref, s_ref, below_ref, above_ref, one_ref, two_ref, one_late_ref, two_late_ref):
    pack = functools.partial(pack_x, f_ref, s_ref, below_ref, above_ref)
    by_side((one_ref, one_late_ref), (two_ref, two_late_ref), pack)


def pack_x(f_ref, s_ref, below_ref, above_ref, left, right):
    xl_ref, xr_ref = left[0], right[0]
    pack_x_fields(4, f_ref, below_ref, above_ref, xl_ref, xr_ref)
    lowm = low(8)
    m_below, m_above = y_masks()
    for ra in range(18):
        below = below_ref[pl.ds(NF + ra * 8, 8), :] * m_below
        above = above_ref[pl.ds(NF + ra * 8, 8), :] * m_above
        for l in range(0, L, 2):
            row = ra * L + l
            v = [add_y(s_ref[pl.ds((row + i) * 8, 8), :], l + i, below, above, lowm) for i in range(2)]
            if ra < 9:
                put_pair(xl_ref, xr_ref, XF + row * 4, v[0], v[1])
            else:
                put_pair(left[1], right[1], row * 4 - XS, v[0], v[1])


def pack_x2_kernel(f_ref, below_ref, above_ref, one_ref, two_ref):
    by_side(one_ref, two_ref, functools.partial(pack_x_fields, 3, f_ref, below_ref, above_ref))


def v_row(cls, shifted, comp, ext):
    return PAD + (((cls * 2 + shifted) * 4 + comp) * 8 + ext) * 8


def fill_class(v_ref, cls, pz, comp, v):
    low_edge = pz == 1
    if isinstance(pz, int):
        shift, edge = (1, 0) if low_edge else (127, 63)
        shift_swap = (shift + 64) % 128
    else:
        shift, edge = jnp.where(low_edge, 1, 127), jnp.where(low_edge, 0, 63)
        shift_swap = jnp.where(low_edge, 65, 63)
    keep = (lanes(8) & 63) != edge
    base = v_row(cls, 0, comp, 0)
    moved = v_row(cls, 1, comp, 0)
    for l in (0, L - 1):
        ext = 56 if l == 0 else 0
        v_ref[pl.ds(base + ext, 8), :] = swap(v[l])
        v_ref[pl.ds(moved + ext, 8), :] = jnp.where(keep, pltpu.roll(v[l], shift_swap, 1), 0.0)
    for l in range(L):
        v_ref[pl.ds(moved + (l + 1) * 8, 8), :] = jnp.where(keep, pltpu.roll(v[l], shift, 1), 0.0)


def fill_all(comps, v_ref):
    for comp in range(comps):
        for cls in range(8):
            base = v_row(cls, 0, comp, 1)
            fill_class(v_ref, cls, cls & 1, comp, [v_ref[pl.ds(base + l * 8, 8), :] for l in range(L)])


def place_own(comps, v_ref, e_ref, xl_ref, xr_ref):
    zero = jnp.zeros((8, 128), F32)
    sub = lax.broadcasted_iota(jnp.int32, (8, 128), 0) < 4
    for comp in range(comps):
        for l in range(L):
            for p in (0, 2):
                row = ((comp * L + l) * 4 + p) * 4
                a, b = xl_ref[pl.ds(row, 8), :], xr_ref[pl.ds(row, 8), :]
                at = (l * 4 + p) * 16
                e_ref[pl.ds(at + 4, 8), :] = jnp.where(sub, a, pltpu.roll(b, 4, 0))
                e_ref[pl.ds(at + 20, 8), :] = jnp.where(sub, pltpu.roll(a, 4, 0), b)
        for l in range(L):
            for p in range(4):
                for px in range(2):
                    v_ref[pl.ds(v_row(px * 4 + p, 0, comp, l + 1), 8), :] = e_ref[
                        pl.ds((l * 4 + p) * 16 + px, 8, stride=2), :
                    ]


def place_ghosts(comps, v_ref, rl_ref, rr_ref):
    m_left, m_right = x_masks()
    for comp in range(comps):
        for p in range(4):
            for px in range(2):
                base = v_row(px * 4 + p, 0, comp, 1)
                for i in range(2):
                    row = (comp * L * 4 + p) * 4 + px + 2 * i
                    v_ref[pl.ds(base + i, L, stride=8), :] = rl_ref[pl.ds(row, L, stride=16), :] * m_left
                    v_ref[pl.ds(base + 6 + i, L, stride=8), :] = rr_ref[pl.ds(row, L, stride=16), :] * m_right


def place_own_statics(r, base, st_ref, xl_ref, xr_ref, own_ref, below_ref, above_ref):
    m_below, m_above = y_masks()
    lowm = low(1)
    zero = jnp.zeros((8, 128), F32)
    for a in range(9):
        below = below_ref[pl.ds(NF + (r * 9 + a) * 8, 8), :] * m_below
        above = above_ref[pl.ds(NF + (r * 9 + a) * 8, 8), :] * m_above
        for l in range(L):
            srow = base + (a * L + l) * 4
            own_l, own_r = xl_ref[pl.ds(srow, 4), :], xr_ref[pl.ds(srow, 4), :]
            at = (a * L + l) * 8
            st_ref[pl.ds(at, 8), :] = zero
            st_ref[pl.ds(at + 2, 2), :] = own_l[0:2]
            st_ref[pl.ds(at + 4, 2), :] = own_r[0:2]
            for k in (1, 2, 3):
                at = ((k * 9 + a) * L + l) * 8
                st_ref[pl.ds(at, 8), :] = zero
                st_ref[pl.ds(at + 2, 4), :] = own_ref[pl.ds((((k - 1) * 9 + a) * L + l) * 4, 4), :]
                if k < 3:
                    st_ref[pl.ds(at + 2, 1), :] = own_l[1 + k : 2 + k]
                    st_ref[pl.ds(at + 5, 1), :] = own_r[1 + k : 2 + k]
                    for q in range(2):
                        at_q = at + 3 + q
                        if l == 1:
                            st_ref[pl.ds(at_q, 1), :] = jnp.where(
                                lowm, below[1 + k + 4 * q : 2 + k + 4 * q], st_ref[pl.ds(at_q, 1), :]
                            )
                        if l == 4:
                            st_ref[pl.ds(at_q, 1), :] = jnp.where(
                                lowm, st_ref[pl.ds(at_q, 1), :], above[1 + k + 4 * q : 2 + k + 4 * q]
                            )


def place_ghost_statics(base_row, st_ref, rl_ref, rr_ref):
    m_left, m_right = x_masks()
    for a in range(9):
        for row, k, at_l, at_r in ((0, 0, 0, 6), (1, 0, 1, 7), (2, 1, 1, 6), (3, 2, 1, 6)):
            src = pl.ds(base_row + a * L * 4 + row, L, stride=4)
            base = (k * 9 + a) * L * 8
            st_ref[pl.ds(base + at_l, L, stride=8), :] = rl_ref[src, :] * m_left
            st_ref[pl.ds(base + at_r, L, stride=8), :] = rr_ref[src, :] * m_right


def relax(cls, k, v_ref, st_ref, stencil_ref):
    px, py, pz = parity(cls)
    by_x = {0: 0, -1: px - 1, 1: px}
    by_y = {0: 0, -1: (py - 1) * 8, 1: py * 8}
    by_z = {0: 0, -1: 1 - pz, 1: pz}
    centre = [v_ref[pl.ds(v_row(cls, 0, 3, l + 1), 8), :] for l in range(L)]
    acc = [[None] * L for _ in range(3)]
    fresh = [[None] * L for _ in range(3)]
    for number, (a, b, c) in enumerate(offsets):
        for orient in (1, -1):
            da, db, dc = orient * a, orient * b, orient * c
            source = cls ^ (4 * abs(a) + 2 * abs(b) + abs(c))
            base = v_row(source, by_z[dc], 0, 1) + by_y[db] + by_x[da]
            block = [
                [stencil_ref[number * 9 + (i * 3 + j if orient == 1 else j * 3 + i)] for j in range(3)]
                for i in range(3)
            ]
            for l in range(L):
                weight = centre[l] + v_ref[pl.ds(base + 3 * 64 + l * 8, 8), :]
                wu = [weight * v_ref[pl.ds(base + j * 64 + l * 8, 8), :] for j in range(3)]
                for i in range(3):
                    term = block[i][0] * wu[0] + block[i][1] * wu[1] + block[i][2] * wu[2]
                    acc[i][l] = term if acc[i][l] is None else acc[i][l] + term
    for l in range(L):
        s = [st_ref[pl.ds(((k * 9 + a) * L + l) * 8, 8), :] for a in range(9)]
        rest = [s[i] - acc[i][l] for i in range(3)]
        inv = ((s[3], s[4], s[5]), (s[4], s[6], s[7]), (s[5], s[7], s[8]))
        for i in range(3):
            fresh[i][l] = inv[i][0] * rest[0] + inv[i][1] * rest[1] + inv[i][2] * rest[2]
            v_ref[pl.ds(v_row(cls, 0, i, l + 1), 8), :] = fresh[i][l]

    @pl.when(k < 3)
    def _():
        for i in range(3):
            fill_class(v_ref, cls, pz, i, fresh[i])


def four_colours(r, order_ref, v_ref, st_ref, stencil_ref):
    @pl.loop(0, 4)
    def _(k):
        relax(order_ref[4 * r + k], k, v_ref, st_ref, stencil_ref)


VROWS = 2 * PAD + 8 * 2 * 4 * 64
STROWS = 4 * 9 * L * 8


def prepare_kernel(one_ref, two_ref, own_ref, below_ref, above_ref, v_ref, st_ref, e_ref):
    v_ref[pl.ds(0, PAD), :] = jnp.zeros((PAD, 128), F32)
    v_ref[pl.ds(VROWS - PAD, PAD), :] = jnp.zeros((PAD, 128), F32)

    def place(xl_ref, xr_ref):
        place_own(4, v_ref, e_ref, xl_ref, xr_ref)
        place_own_statics(0, XF, st_ref, xl_ref, xr_ref, own_ref, below_ref, above_ref)

    by_side(one_ref, two_ref, place)


def first_kernel(order_ref, stencil_ref, two_ref, one_ref, _v, _st, v_ref, st_ref, lo_ref, hi_ref):

    def place(rl_ref, rr_ref):
        place_ghosts(4, v_ref, rl_ref, rr_ref)
        place_ghost_statics(XF, st_ref, rl_ref, rr_ref)

    by_side(one_ref, two_ref, place)
    fill_all(4, v_ref)
    four_colours(0, order_ref, v_ref, st_ref, stencil_ref)
    lowm = low(4)
    for comp in range(3):
        for p in range(4):
            for px in range(2):
                at = v_row(px * 4 + p, 0, comp, 3) + 2
                v2, v3 = v_ref[pl.ds(at, 4), :], v_ref[pl.ds(at + 8, 4), :]
                to = pl.ds((comp * 4 + p) * 8 + px, 4, stride=2)
                lo_ref[to, :] = jnp.where(lowm, v2, swap(v3))
                hi_ref[to, :] = jnp.where(lowm, swap(v2), v3)


def between_kernel(v_ref, r1_ref, x1_ref, x2_ref, r2_ref, own_ref, below_ref, above_ref, f_ref, st_ref):
    for comp in range(3):
        for l in range(L):
            for p in range(4):
                for px in range(2):
                    f_ref[pl.ds(((comp * L + l) * 4 + p) * 8 + px, 4, stride=2), :] = v_ref[
                        pl.ds(v_row(px * 4 + p, 0, comp, l + 1) + 2, 4), :
                    ]

    def place(left, right):
        place_own_statics(1, 0, st_ref, left[0], right[0], own_ref, below_ref, above_ref)
        place_ghost_statics(0, st_ref, left[1], right[1])

    by_side((x1_ref, r1_ref), (x2_ref, r2_ref), place)


def prepare2_kernel(one_ref, two_ref, _v, v_ref, e_ref):
    by_side(one_ref, two_ref, functools.partial(place_own, 3, v_ref, e_ref))


def second_kernel(order_ref, stencil_ref, two_ref, one_ref, st_ref, _v, v_ref, out_ref):
    by_side(one_ref, two_ref, functools.partial(place_ghosts, 3, v_ref))
    fill_all(3, v_ref)
    four_colours(1, order_ref, v_ref, st_ref, stencil_ref)
    lowm = low(4)
    lane = lanes(4)
    merge = lax.shift_right_logical(lane, 1) + 64 * (lane & 1)
    for comp in range(3):
        for px in range(2):
            for py in range(2):
                cls = px * 4 + py * 2
                for l in range(L):
                    ev = v_ref[pl.ds(v_row(cls, 0, comp, l + 1) + 2, 4), :]
                    od = v_ref[pl.ds(v_row(cls + 1, 0, comp, l + 1) + 2, 4), :]
                    first = comp * 128 + px * 16 + py
                    if l >= 2:
                        out_ref[pl.ds(first + 2 * (l - 2), 4, stride=32), :] = gather(
                            jnp.where(lowm, ev, swap(od)), merge
                        )
                    if l <= 3:
                        out_ref[pl.ds(first + 2 * (l + 4), 4, stride=32), :] = gather(
                            jnp.where(lowm, swap(ev), od), merge
                        )


SMEM = pl.BlockSpec(memory_space=pltpu.SMEM)
VMEM = pl.BlockSpec(memory_space=pltpu.VMEM)


HBM = pl.BlockSpec(memory_space=pltpu.HBM)


def call(kernel, specs, outs, scratch, cost, aliases={}, vmem=24, extra_outs=(), extra_out_specs=(), extra_scratch=()):
    return pl.pallas_call(
        kernel,
        in_specs=specs,
        out_shape=tuple(jax.ShapeDtypeStruct((n, 128), F32) for n in outs) + tuple(extra_outs),
        out_specs=tuple(VMEM for _ in outs) + tuple(extra_out_specs),
        scratch_shapes=[pltpu.VMEM((n, 128), F32) for n in scratch] + list(extra_scratch),
        input_output_aliases=aliases,
        compiler_params=pltpu.CompilerParams(vmem_limit_bytes=vmem * 1024 * 1024),
        cost_estimate=pl.CostEstimate(flops=cost, bytes_accessed=cost, transcendentals=0),
    )


def ring(value, axis, step):
    count = lax.axis_size(axis)
    return lax.ppermute(value, axis, [(i, (i + step) % count) for i in range(count)])


def swaps(one, two):
    n = lax.axis_size("gx")
    first = [(i, i ^ 1) for i in range(n)]
    second = [(i, (i + 1 if i % 2 else i - 1) % n) for i in range(n)]
    far = lax.ppermute(two, "gx", second)
    return lax.ppermute(one, "gx", first), far


def per_device(displacement, load_vector, diag_inverse, stiffness, stencil, colour):
    disp = displacement.reshape(3 * 128, 128)
    load = load_vector.reshape(3 * 128, 128)
    inv = diag_inverse.reshape(9 * 128, 128)
    stiff = stiffness.reshape(128, 128)
    colours = colour.reshape(128, 128)
    coefs = stencil.reshape(117)

    lo, hi, order, nat = call(
        pack_y_kernel,
        [HBM] * 5,
        (NF + NS, NF + NS),
        (NAT_ROWS,),
        1 << 20,
        vmem=56,
        extra_outs=[jax.ShapeDtypeStruct((8,), jnp.int32), jax.ShapeDtypeStruct((NAT_ROWS, 128), F32)],
        extra_out_specs=[SMEM, HBM],
        extra_scratch=[pltpu.SMEM((16, 128), jnp.int32), pltpu.SemaphoreType.DMA((12,))],
    )(colours, disp, load, inv, stiff)
    above = ring(lo, "gy", -1)
    below = ring(hi, "gy", 1)
    f, s, own0, own1 = call(convert_kernel, [VMEM], (768, 864, 648, 648), (), 1 << 22)(nat)
    x1, x2, late1, late2 = call(pack_x_kernel, [VMEM] * 4, (XF + XS, XF + XS, XS, XS), (), 1 << 20)(f, s, below, above)
    r1, r2 = swaps(x1, x2)
    got1, got2 = swaps(late1, late2)
    v, st = call(prepare_kernel, [VMEM] * 5, (VROWS, STROWS), (384,), 1 << 22)(x1, x2, own0, below, above)
    v, _, lo2, hi2 = call(
        first_kernel, [SMEM] * 2 + [VMEM] * 4, (VROWS, STROWS, 96, 96), (), 1 << 24, aliases={4: 0, 5: 1}
    )(order, coefs, r2, r1, v, st)
    above2 = ring(lo2, "gy", -1)
    below2 = ring(hi2, "gy", 1)
    f2, st = call(between_kernel, [VMEM] * 8, (576, STROWS), (), 1 << 22)(v, got1, late1, late2, got2, own1, below, above)
    x1, x2 = call(pack_x2_kernel, [VMEM] * 3, (288, 288), (), 1 << 20)(f2, below2, above2)
    r1, r2 = swaps(x1, x2)
    (v,) = call(prepare2_kernel, [VMEM] * 3, (VROWS,), (384,), 1 << 22, aliases={2: 0})(x1, x2, v)
    v, out = call(second_kernel, [SMEM] * 2 + [VMEM] * 4, (VROWS, 384), (), 1 << 24, aliases={5: 0})(
        order, coefs, r2, r1, st, v
    )
    return out.reshape(3, XD, YD, ZD)


def solution(mesh):
    return jax.shard_map(
        per_device,
        mesh=mesh,
        in_specs=(
            P(None, "gx", "gy", None),
            P(None, "gx", "gy", None),
            P(None, None, "gx", "gy", None),
            P("gx", "gy", None),
            P(),
            P("gx", "gy", None),
        ),
        out_specs=P(None, "gx", "gy", None),
        check_vma=False,
    )
```

```python
import functools

import jax
import jax.numpy as jnp
from jax import lax
from jax.experimental import pallas as pl
from jax.experimental.pallas import tpu as pltpu
from jax.sharding import PartitionSpec as P

XD, YD, ZD = 8, 16, 128
L = 6
PAD = 8
F32 = jnp.float32

offsets = [
    (a, b, c)
    for a in (-1, 0, 1)
    for b in (-1, 0, 1)
    for c in (-1, 0, 1)
    if (a, b, c) > (0, 0, 0)
]

NF = 16 * 8
NS = 9 * 8
XF = 4 * L * 4 * 4
XS = 9 * L * 4


def lanes(rows):
    return lax.broadcasted_iota(jnp.int32, (rows, 128), 1)


def low(rows):
    return lanes(rows) < 64


def gather(v, idx):
    return jnp.take_along_axis(v, idx, axis=1, mode="promise_in_bounds")


def split_idx(rows, first):
    lane = lanes(rows)
    return jnp.where(lane < 64, 2 * lane + first, 2 * lane - 127 - first)


def swap(v):
    return pltpu.roll(v, 64, 1)


def parity(cls):
    return lax.shift_right_logical(cls, 2), lax.shift_right_logical(cls, 1) & 1, cls & 1


def load_rows(nat, first, cls_row, y1, count):
    return nat[pl.ds(first + cls_row + 2 * y1, count, stride=32), :]


NAT_LOAD, NAT_INV, NAT_STIFF, NAT_ORDER, NAT_ROWS = 384, 768, 1536, 1664, 1672


def static_rows():
    return [NAT_LOAD + i * 128 for i in range(3)] + [NAT_INV + i * 128 for i in range(6)]


def field_rows():
    return [0, 128, 256, NAT_STIFF]


def pack_y_kernel(
    colour_hbm, disp_hbm, load_hbm, inv_hbm, stiff_hbm,
    lo_ref, hi_ref, lo_late_ref, hi_late_ref, order_ref, nat_hbm, nat_ref, colour_s, sems,
):
    moves = [
        (colour_hbm.at[pl.ds(0, 8)], colour_s.at[pl.ds(0, 8)]),
        (colour_hbm.at[pl.ds(16, 8)], colour_s.at[pl.ds(8, 8)]),
        (disp_hbm, nat_ref.at[pl.ds(0, 384)]),
        (stiff_hbm, nat_ref.at[pl.ds(NAT_STIFF, 128)]),
        (load_hbm, nat_ref.at[pl.ds(NAT_LOAD, 384)]),
        (inv_hbm.at[pl.ds(0, 384)], nat_ref.at[pl.ds(NAT_INV, 384)]),
        (inv_hbm.at[pl.ds(512, 256)], nat_ref.at[pl.ds(NAT_INV + 384, 256)]),
        (inv_hbm.at[pl.ds(1024, 128)], nat_ref.at[pl.ds(NAT_INV + 640, 128)]),
    ]
    copies = [pltpu.make_async_copy(a, b, sems.at[i]) for i, (a, b) in enumerate(moves)]
    for copy in copies:
        copy.start()

    def keep(first, count, i):
        part = pl.ds(first, count)
        copy = pltpu.make_async_copy(nat_ref.at[part], nat_hbm.at[part], sems.at[8 + i])
        copy.start()
        return copy

    copies[2].wait()
    copies[3].wait()
    kept = [keep(0, 384, 0), keep(NAT_STIFF, 128, 1)]
    lowm = low(8)
    idx_e = split_idx(8, 0)
    for comp, first in enumerate(field_rows()):
        for py in range(2):
            for out, y1 in ((lo_ref, 0), (hi_ref, 6)):
                a = nat_ref[pl.ds(first + py + 2 * y1, 8, stride=16), :]
                b = nat_ref[pl.ds(first + py + 2 * y1 + 2, 8, stride=16), :]
                if comp == 3:
                    a, b = 0.5 * a, 0.5 * b
                a, b = gather(a, idx_e), gather(b, idx_e)
                row = (comp * 4 + py * 2) * 8
                out[pl.ds(row, 8), :] = jnp.where(lowm, a, swap(b))
                out[pl.ds(row + 8, 8), :] = jnp.where(lowm, swap(a), b)
    copies[0].wait()
    copies[1].wait()
    for cls in range(8):
        px, py, pz = cls >> 2, (cls >> 1) & 1, cls & 1
        order_ref[colour_s[8 * px + py, pz]] = cls
    for k in range(8):
        nat_ref[pl.ds(NAT_ORDER + k, 1), :] = jnp.full((1, 128), order_ref[k].astype(F32))
    kept.append(keep(NAT_ORDER, 8, 3))
    for copy in copies[4:]:
        copy.wait()
    kept.append(keep(NAT_LOAD, 1152, 2))
    sub = lax.broadcasted_iota(jnp.int32, (8, 128), 0)
    second, third, upper = (sub & 3) == 2, (sub & 3) == 3, sub >= 4

    def rows(start, stride):
        return nat_ref[pl.ds(start, 8, stride=stride), :]

    for r in range(2):
        px, py, pz = zip(*[parity(order_ref[4 * r + k]) for k in range(3)])
        cls_row = [px[k] * 16 + py[k] for k in range(3)]
        idx = 2 * (lanes(8) & 63) + jnp.where(second, pz[1], jnp.where(third, pz[2], pz[0]))
        for side, out in enumerate(((lo_ref, hi_ref), (lo_late_ref, hi_late_ref))[r]):
            near, far = (0, 1) if side == 0 else (7, 6)
            for a, first in enumerate(static_rows()):
                at = [first + 2 * near + cls_row[k] for k in range(3)]
                at_far = first + 2 * far + cls_row[0]
                nv = jnp.where(upper, rows(at[0] - 64, 32), rows(at[0], 32))
                nv = jnp.where(second, rows(at[1] - 48, 24), jnp.where(third, rows(at[2] - 72, 24), nv))
                fv = jnp.where(upper, rows(at_far - 64, 32), rows(at_far, 32))
                fv = jnp.where(second, rows(at[1] + 16, 8), jnp.where(third, rows(at[2] + 8, 8), fv))
                nv, fv = gather(nv, idx), gather(fv, idx)
                out[pl.ds((NF if r == 0 else 0) + a * 8, 8), :] = (
                    jnp.where(lowm, nv, fv) if side == 0 else jnp.where(lowm, fv, nv)
                )
    for copy in kept:
        copy.wait()


def convert_kernel(nat_ref, f_ref, s_ref, own0_ref, own1_ref):
    lowm = low(8)
    low4 = low(4)
    idx_e = split_idx(8, 0)
    zero = jnp.zeros((8, 128), F32)
    for comp, first in enumerate(field_rows()):
        for py in range(2):
            ev, od = [], []
            for y1 in range(8):
                v = nat_ref[pl.ds(first + py + 2 * y1, 8, stride=16), :]
                if comp == 3:
                    v = 0.5 * v
                v = gather(v, idx_e)
                ev.append(v)
                od.append(swap(v))
            for l in range(L):
                e0, o0 = (ev[l - 2], od[l - 2]) if l >= 2 else (zero, zero)
                e1, o1 = (ev[l + 4], od[l + 4]) if l <= 3 else (zero, zero)
                row = ((comp * L + l) * 4 + py * 2) * 8
                f_ref[pl.ds(row, 8), :] = jnp.where(lowm, e0, o1)
                f_ref[pl.ds(row + 8, 8), :] = jnp.where(lowm, o0, e1)
    zero4 = jnp.zeros((4, 128), F32)
    for r, own in ((0, own0_ref), (1, own1_ref)):
        for k in range(4):
            px, py, pz = parity(nat_ref[NAT_ORDER + 4 * r + k, 0].astype(jnp.int32))
            cls_row = px * 16 + py
            idx0, idx1 = split_idx(4, pz), split_idx(4, 1 - pz)
            for a, first in enumerate(static_rows()):
                rows = [load_rows(nat_ref, first, cls_row, y1, 4) for y1 in range(8)]
                for l in range(L):
                    v0 = gather(rows[l - 2], idx0) if l >= 2 else zero4
                    v1 = gather(rows[l + 4], idx1) if l <= 3 else zero4
                    v = jnp.where(low4, v0, v1)
                    srow = ((r * 9 + a) * L + l) * 8
                    if k == 0:
                        s_ref[pl.ds(srow, 2), :] = v[0:2]
                        s_ref[pl.ds(srow + 4, 2), :] = v[2:4]
                    else:
                        own[pl.ds((((k - 1) * 9 + a) * L + l) * 4, 4), :] = v
                        if k < 3:
                            s_ref[pl.ds(srow + 1 + k, 1), :] = v[0:1]
                            s_ref[pl.ds(srow + 5 + k, 1), :] = v[3:4]


def add_y(v, l, below, above, lowm):
    if l == 0:
        return jnp.where(lowm, below, v)
    if l == 1:
        return jnp.where(lowm, swap(below), v)
    if l == 4:
        return jnp.where(lowm, v, swap(above))
    if l == 5:
        return jnp.where(lowm, v, above)
    return v


def put_pair(xl_ref, xr_ref, row, v, w):
    sub = lax.broadcasted_iota(jnp.int32, (8, 128), 0) < 4
    xl_ref[pl.ds(row, 8), :] = jnp.where(sub, v, pltpu.roll(w, 4, 0))
    xr_ref[pl.ds(row, 8), :] = jnp.where(sub, pltpu.roll(v, 4, 0), w)


def by_side(one, two, run):
    even = lax.axis_index("gx") % 2 == 0

    @pl.when(even)
    def _():
        run(two, one)

    @pl.when(jnp.logical_not(even))
    def _():
        run(one, two)


def y_masks():
    gy = lax.axis_index("gy")
    return (
        jnp.where(gy > 0, 1.0, 0.0).astype(F32),
        jnp.where(gy < lax.axis_size("gy") - 1, 1.0, 0.0).astype(F32),
    )


def x_masks():
    gx = lax.axis_index("gx")
    return (
        jnp.where(gx > 0, 1.0, 0.0).astype(F32),
        jnp.where(gx < lax.axis_size("gx") - 1, 1.0, 0.0).astype(F32),
    )


def pack_x_fields(comps, f_ref, below_ref, above_ref, xl_ref, xr_ref):
    lowm = low(8)
    m_below, m_above = y_masks()
    for comp in range(comps):
        for half in range(2):
            below = [below_ref[pl.ds((comp * 4 + 2 * half + i) * 8, 8), :] * m_below for i in range(2)]
            above = [above_ref[pl.ds((comp * 4 + 2 * half + i) * 8, 8), :] * m_above for i in range(2)]
            for l in range(L):
                row = (comp * L + l) * 4 + 2 * half
                v = [add_y(f_ref[pl.ds((row + i) * 8, 8), :], l, below[i], above[i], lowm) for i in range(2)]
                put_pair(xl_ref, xr_ref, row * 4, v[0], v[1])


def pack_x_statics(y_base, x_base, s_base, s_ref, below_ref, above_ref, xl_ref, xr_ref):
    lowm = low(8)
    m_below, m_above = y_masks()
    for a in range(9):
        below = below_ref[pl.ds(y_base + a * 8, 8), :] * m_below
        above = above_ref[pl.ds(y_base + a * 8, 8), :] * m_above
        for l in range(0, L, 2):
            row = a * L + l
            v = [add_y(s_ref[pl.ds(s_base + (row + i) * 8, 8), :], l + i, below, above, lowm) for i in range(2)]
            put_pair(xl_ref, xr_ref, x_base + row * 4, v[0], v[1])


def pack_x_kernel(f_ref, s_ref, below_ref, above_ref, one_ref, two_ref):
    def pack(xl_ref, xr_ref):
        pack_x_fields(4, f_ref, below_ref, above_ref, xl_ref, xr_ref)
        pack_x_statics(NF, XF, 0, s_ref, below_ref, above_ref, xl_ref, xr_ref)

    by_side(one_ref, two_ref, pack)


def pack_late_kernel(s_ref, below_ref, above_ref, one_ref, two_ref):
    by_side(one_ref, two_ref, functools.partial(pack_x_statics, 0, 0, 9 * L * 8, s_ref, below_ref, above_ref))


def pack_x2_kernel(f_ref, below_ref, above_ref, one_ref, two_ref):
    by_side(one_ref, two_ref, functools.partial(pack_x_fields, 3, f_ref, below_ref, above_ref))


def v_row(cls, shifted, comp, ext):
    return PAD + (((cls * 2 + shifted) * 4 + comp) * 8 + ext) * 8


def fill_class(v_ref, cls, pz, comp, v):
    low_edge = pz == 1
    if isinstance(pz, int):
        shift, edge = (1, 0) if low_edge else (127, 63)
        shift_swap = (shift + 64) % 128
    else:
        shift, edge = jnp.where(low_edge, 1, 127), jnp.where(low_edge, 0, 63)
        shift_swap = jnp.where(low_edge, 65, 63)
    keep = (lanes(8) & 63) != edge
    base = v_row(cls, 0, comp, 0)
    moved = v_row(cls, 1, comp, 0)
    for l in (0, L - 1):
        ext = 56 if l == 0 else 0
        v_ref[pl.ds(base + ext, 8), :] = swap(v[l])
        v_ref[pl.ds(moved + ext, 8), :] = jnp.where(keep, pltpu.roll(v[l], shift_swap, 1), 0.0)
    for l in range(L):
        v_ref[pl.ds(moved + (l + 1) * 8, 8), :] = jnp.where(keep, pltpu.roll(v[l], shift, 1), 0.0)


def fill_all(comps, v_ref):
    for comp in range(comps):
        for cls in range(8):
            base = v_row(cls, 0, comp, 1)
            fill_class(v_ref, cls, cls & 1, comp, [v_ref[pl.ds(base + l * 8, 8), :] for l in range(L)])


def place_own(comps, v_ref, e_ref, xl_ref, xr_ref):
    zero = jnp.zeros((8, 128), F32)
    sub = lax.broadcasted_iota(jnp.int32, (8, 128), 0) < 4
    for comp in range(comps):
        for l in range(L):
            for p in (0, 2):
                row = ((comp * L + l) * 4 + p) * 4
                a, b = xl_ref[pl.ds(row, 8), :], xr_ref[pl.ds(row, 8), :]
                at = (l * 4 + p) * 16
                e_ref[pl.ds(at + 4, 8), :] = jnp.where(sub, a, pltpu.roll(b, 4, 0))
                e_ref[pl.ds(at + 20, 8), :] = jnp.where(sub, pltpu.roll(a, 4, 0), b)
        for l in range(L):
            for p in range(4):
                for px in range(2):
                    v_ref[pl.ds(v_row(px * 4 + p, 0, comp, l + 1), 8), :] = e_ref[
                        pl.ds((l * 4 + p) * 16 + px, 8, stride=2), :
                    ]


def place_ghosts(comps, v_ref, rl_ref, rr_ref):
    m_left, m_right = x_masks()
    for comp in range(comps):
        for p in range(4):
            for px in range(2):
                base = v_row(px * 4 + p, 0, comp, 1)
                for i in range(2):
                    row = (comp * L * 4 + p) * 4 + px + 2 * i
                    v_ref[pl.ds(base + i, L, stride=8), :] = rl_ref[pl.ds(row, L, stride=16), :] * m_left
                    v_ref[pl.ds(base + 6 + i, L, stride=8), :] = rr_ref[pl.ds(row, L, stride=16), :] * m_right


def place_own_statics(r, base, st_ref, xl_ref, xr_ref, own_ref, below_ref, above_ref):
    m_below, m_above = y_masks()
    lowm = low(1)
    zero = jnp.zeros((8, 128), F32)
    for a in range(9):
        below = below_ref[pl.ds((NF if r == 0 else 0) + a * 8, 8), :] * m_below
        above = above_ref[pl.ds((NF if r == 0 else 0) + a * 8, 8), :] * m_above
        for l in range(L):
            srow = base + (a * L + l) * 4
            own_l, own_r = xl_ref[pl.ds(srow, 4), :], xr_ref[pl.ds(srow, 4), :]
            at = (a * L + l) * 8
            st_ref[pl.ds(at, 8), :] = zero
            st_ref[pl.ds(at + 2, 2), :] = own_l[0:2]
            st_ref[pl.ds(at + 4, 2), :] = own_r[0:2]
            for k in (1, 2, 3):
                at = ((k * 9 + a) * L + l) * 8
                st_ref[pl.ds(at, 8), :] = zero
                st_ref[pl.ds(at + 2, 4), :] = own_ref[pl.ds((((k - 1) * 9 + a) * L + l) * 4, 4), :]
                if k < 3:
                    st_ref[pl.ds(at + 2, 1), :] = own_l[1 + k : 2 + k]
                    st_ref[pl.ds(at + 5, 1), :] = own_r[1 + k : 2 + k]
                    for q in range(2):
                        at_q = at + 3 + q
                        if l == 1:
                            st_ref[pl.ds(at_q, 1), :] = jnp.where(
                                lowm, below[1 + k + 4 * q : 2 + k + 4 * q], st_ref[pl.ds(at_q, 1), :]
                            )
                        if l == 4:
                            st_ref[pl.ds(at_q, 1), :] = jnp.where(
                                lowm, st_ref[pl.ds(at_q, 1), :], above[1 + k + 4 * q : 2 + k + 4 * q]
                            )


def place_ghost_statics(base_row, st_ref, rl_ref, rr_ref):
    m_left, m_right = x_masks()
    for a in range(9):
        for row, k, at_l, at_r in ((0, 0, 0, 6), (1, 0, 1, 7), (2, 1, 1, 6), (3, 2, 1, 6)):
            src = pl.ds(base_row + a * L * 4 + row, L, stride=4)
            base = (k * 9 + a) * L * 8
            st_ref[pl.ds(base + at_l, L, stride=8), :] = rl_ref[src, :] * m_left
            st_ref[pl.ds(base + at_r, L, stride=8), :] = rr_ref[src, :] * m_right


def relax(cls, k, v_ref, st_ref, stencil_ref):
    px, py, pz = parity(cls)
    by_x = {0: 0, -1: px - 1, 1: px}
    by_y = {0: 0, -1: (py - 1) * 8, 1: py * 8}
    by_z = {0: 0, -1: 1 - pz, 1: pz}
    centre = [v_ref[pl.ds(v_row(cls, 0, 3, l + 1), 8), :] for l in range(L)]
    acc = [[None] * L for _ in range(3)]
    fresh = [[None] * L for _ in range(3)]
    for number, (a, b, c) in enumerate(offsets):
        for orient in (1, -1):
            da, db, dc = orient * a, orient * b, orient * c
            source = cls ^ (4 * abs(a) + 2 * abs(b) + abs(c))
            base = v_row(source, by_z[dc], 0, 1) + by_y[db] + by_x[da]
            block = [
                [stencil_ref[number * 9 + (i * 3 + j if orient == 1 else j * 3 + i)] for j in range(3)]
                for i in range(3)
            ]
            for l in range(L):
                weight = centre[l] + v_ref[pl.ds(base + 3 * 64 + l * 8, 8), :]
                wu = [weight * v_ref[pl.ds(base + j * 64 + l * 8, 8), :] for j in range(3)]
                for i in range(3):
                    term = block[i][0] * wu[0] + block[i][1] * wu[1] + block[i][2] * wu[2]
                    acc[i][l] = term if acc[i][l] is None else acc[i][l] + term
    for l in range(L):
        s = [st_ref[pl.ds(((k * 9 + a) * L + l) * 8, 8), :] for a in range(9)]
        rest = [s[i] - acc[i][l] for i in range(3)]
        inv = ((s[3], s[4], s[5]), (s[4], s[6], s[7]), (s[5], s[7], s[8]))
        for i in range(3):
            fresh[i][l] = inv[i][0] * rest[0] + inv[i][1] * rest[1] + inv[i][2] * rest[2]
            v_ref[pl.ds(v_row(cls, 0, i, l + 1), 8), :] = fresh[i][l]

    @pl.when(k < 3)
    def _():
        for i in range(3):
            fill_class(v_ref, cls, pz, i, fresh[i])


def four_colours(r, order_ref, v_ref, st_ref, stencil_ref):
    @pl.loop(0, 4)
    def _(k):
        relax(order_ref[4 * r + k], k, v_ref, st_ref, stencil_ref)


VROWS = 2 * PAD + 8 * 2 * 4 * 64
STROWS = 4 * 9 * L * 8


def prepare_kernel(one_ref, two_ref, own_ref, below_ref, above_ref, v_ref, st_ref, e_ref):
    v_ref[pl.ds(0, PAD), :] = jnp.zeros((PAD, 128), F32)
    v_ref[pl.ds(VROWS - PAD, PAD), :] = jnp.zeros((PAD, 128), F32)

    def place(xl_ref, xr_ref):
        place_own(4, v_ref, e_ref, xl_ref, xr_ref)
        place_own_statics(0, XF, st_ref, xl_ref, xr_ref, own_ref, below_ref, above_ref)

    by_side(one_ref, two_ref, place)


def first_kernel(order_ref, stencil_ref, two_ref, one_ref, _v, _st, v_ref, st_ref, lo_ref, hi_ref):

    def place(rl_ref, rr_ref):
        place_ghosts(4, v_ref, rl_ref, rr_ref)
        place_ghost_statics(XF, st_ref, rl_ref, rr_ref)

    by_side(one_ref, two_ref, place)
    fill_all(4, v_ref)
    four_colours(0, order_ref, v_ref, st_ref, stencil_ref)
    lowm = low(4)
    for comp in range(3):
        for p in range(4):
            for px in range(2):
                at = v_row(px * 4 + p, 0, comp, 3) + 2
                v2, v3 = v_ref[pl.ds(at, 4), :], v_ref[pl.ds(at + 8, 4), :]
                to = pl.ds((comp * 4 + p) * 8 + px, 4, stride=2)
                lo_ref[to, :] = jnp.where(lowm, v2, swap(v3))
                hi_ref[to, :] = jnp.where(lowm, swap(v2), v3)


def between_kernel(v_ref, r1_ref, x1_ref, x2_ref, r2_ref, own_ref, below_ref, above_ref, f_ref, st_ref):
    for comp in range(3):
        for l in range(L):
            for p in range(4):
                for px in range(2):
                    f_ref[pl.ds(((comp * L + l) * 4 + p) * 8 + px, 4, stride=2), :] = v_ref[
                        pl.ds(v_row(px * 4 + p, 0, comp, l + 1) + 2, 4), :
                    ]

    def place(left, right):
        place_own_statics(1, 0, st_ref, left[0], right[0], own_ref, below_ref, above_ref)
        place_ghost_statics(0, st_ref, left[1], right[1])

    by_side((x1_ref, r1_ref), (x2_ref, r2_ref), place)


def prepare2_kernel(one_ref, two_ref, _v, v_ref, e_ref):
    by_side(one_ref, two_ref, functools.partial(place_own, 3, v_ref, e_ref))


def second_kernel(order_ref, stencil_ref, two_ref, one_ref, st_ref, _v, v_ref, out_ref):
    by_side(one_ref, two_ref, functools.partial(place_ghosts, 3, v_ref))
    fill_all(3, v_ref)
    four_colours(1, order_ref, v_ref, st_ref, stencil_ref)
    lowm = low(4)
    lane = lanes(4)
    merge = lax.shift_right_logical(lane, 1) + 64 * (lane & 1)
    for comp in range(3):
        for px in range(2):
            for py in range(2):
                cls = px * 4 + py * 2
                for l in range(L):
                    ev = v_ref[pl.ds(v_row(cls, 0, comp, l + 1) + 2, 4), :]
                    od = v_ref[pl.ds(v_row(cls + 1, 0, comp, l + 1) + 2, 4), :]
                    first = comp * 128 + px * 16 + py
                    if l >= 2:
                        out_ref[pl.ds(first + 2 * (l - 2), 4, stride=32), :] = gather(
                            jnp.where(lowm, ev, swap(od)), merge
                        )
                    if l <= 3:
                        out_ref[pl.ds(first + 2 * (l + 4), 4, stride=32), :] = gather(
                            jnp.where(lowm, swap(ev), od), merge
                        )


SMEM = pl.BlockSpec(memory_space=pltpu.SMEM)
VMEM = pl.BlockSpec(memory_space=pltpu.VMEM)


HBM = pl.BlockSpec(memory_space=pltpu.HBM)


def call(kernel, specs, outs, scratch, cost, aliases={}, vmem=24, extra_outs=(), extra_out_specs=(), extra_scratch=()):
    return pl.pallas_call(
        kernel,
        in_specs=specs,
        out_shape=tuple(jax.ShapeDtypeStruct((n, 128), F32) for n in outs) + tuple(extra_outs),
        out_specs=tuple(VMEM for _ in outs) + tuple(extra_out_specs),
        scratch_shapes=[pltpu.VMEM((n, 128), F32) for n in scratch] + list(extra_scratch),
        input_output_aliases=aliases,
        compiler_params=pltpu.CompilerParams(vmem_limit_bytes=vmem * 1024 * 1024),
        cost_estimate=pl.CostEstimate(flops=cost, bytes_accessed=cost, transcendentals=0),
    )


def ring(value, axis, step):
    count = lax.axis_size(axis)
    return lax.ppermute(value, axis, [(i, (i + step) % count) for i in range(count)])


def swaps(one, two):
    n = lax.axis_size("gx")
    first = [(i, i ^ 1) for i in range(n)]
    second = [(i, (i + 1 if i % 2 else i - 1) % n) for i in range(n)]
    far = lax.ppermute(two, "gx", second)
    return lax.ppermute(one, "gx", first), far


def per_device(displacement, load_vector, diag_inverse, stiffness, stencil, colour):
    disp = displacement.reshape(3 * 128, 128)
    load = load_vector.reshape(3 * 128, 128)
    inv = diag_inverse.reshape(9 * 128, 128)
    stiff = stiffness.reshape(128, 128)
    colours = colour.reshape(128, 128)
    coefs = stencil.reshape(117)

    lo, hi, lo_late, hi_late, order, nat = call(
        pack_y_kernel,
        [HBM] * 5,
        (NF + NS, NF + NS, NS, NS),
        (NAT_ROWS,),
        1 << 20,
        vmem=56,
        extra_outs=[jax.ShapeDtypeStruct((8,), jnp.int32), jax.ShapeDtypeStruct((NAT_ROWS, 128), F32)],
        extra_out_specs=[SMEM, HBM],
        extra_scratch=[pltpu.SMEM((16, 128), jnp.int32), pltpu.SemaphoreType.DMA((12,))],
    )(colours, disp, load, inv, stiff)
    above = ring(lo, "gy", -1)
    below = ring(hi, "gy", 1)
    above_late = ring(lo_late, "gy", -1)
    below_late = ring(hi_late, "gy", 1)
    f, s, own0, own1 = call(convert_kernel, [VMEM], (768, 864, 648, 648), (), 1 << 22)(nat)
    x1, x2 = call(pack_x_kernel, [VMEM] * 4, (XF + XS, XF + XS), (), 1 << 20)(f, s, below, above)
    r1, r2 = swaps(x1, x2)
    late1, late2 = call(pack_late_kernel, [VMEM] * 3, (XS, XS), (), 1 << 20)(s, below_late, above_late)
    got1, got2 = swaps(late1, late2)
    v, st = call(prepare_kernel, [VMEM] * 5, (VROWS, STROWS), (384,), 1 << 22)(x1, x2, own0, below, above)
    v, _, lo2, hi2 = call(
        first_kernel, [SMEM] * 2 + [VMEM] * 4, (VROWS, STROWS, 96, 96), (), 1 << 24, aliases={4: 0, 5: 1}
    )(order, coefs, r2, r1, v, st)
    above2 = ring(lo2, "gy", -1)
    below2 = ring(hi2, "gy", 1)
    f2, st = call(between_kernel, [VMEM] * 8, (576, STROWS), (), 1 << 22)(v, got1, late1, late2, got2, own1, below_late, above_late)
    x1, x2 = call(pack_x2_kernel, [VMEM] * 3, (288, 288), (), 1 << 20)(f2, below2, above2)
    r1, r2 = swaps(x1, x2)
    (v,) = call(prepare2_kernel, [VMEM] * 3, (VROWS,), (384,), 1 << 22, aliases={2: 0})(x1, x2, v)
    v, out = call(second_kernel, [SMEM] * 2 + [VMEM] * 4, (VROWS, 384), (), 1 << 24, aliases={5: 0})(
        order, coefs, r2, r1, st, v
    )
    return out.reshape(3, XD, YD, ZD)


def solution(mesh):
    return jax.shard_map(
        per_device,
        mesh=mesh,
        in_specs=(
            P(None, "gx", "gy", None),
            P(None, "gx", "gy", None),
            P(None, None, "gx", "gy", None),
            P("gx", "gy", None),
            P(),
            P("gx", "gy", None),
        ),
        out_specs=P(None, "gx", "gy", None),
        check_vma=False,
    )
```

```python
import functools

import jax
import jax.numpy as jnp
from jax import lax
from jax.experimental import pallas as pl
from jax.experimental.pallas import tpu as pltpu
from jax.sharding import PartitionSpec as P

XD, YD, ZD = 8, 16, 128
L = 6
PAD = 8
F32 = jnp.float32

offsets = [
    (a, b, c)
    for a in (-1, 0, 1)
    for b in (-1, 0, 1)
    for c in (-1, 0, 1)
    if (a, b, c) > (0, 0, 0)
]

NF = 16 * 8
NS = 18 * 8
XF = 4 * L * 4 * 4
XS = 9 * L * 4


def lanes(rows):
    return lax.broadcasted_iota(jnp.int32, (rows, 128), 1)


def low(rows):
    return lanes(rows) < 64


def gather(v, idx):
    return jnp.take_along_axis(v, idx, axis=1, mode="promise_in_bounds")


def split_idx(rows, first):
    lane = lanes(rows)
    return jnp.where(lane < 64, 2 * lane + first, 2 * lane - 127 - first)


def swap(v):
    return pltpu.roll(v, 64, 1)


def parity(cls):
    return lax.shift_right_logical(cls, 2), lax.shift_right_logical(cls, 1) & 1, cls & 1


def load_rows(nat, first, cls_row, y1, count):
    return nat[pl.ds(first + cls_row + 2 * y1, count, stride=32), :]


NAT_LOAD, NAT_INV, NAT_STIFF, NAT_ORDER, NAT_ROWS = 384, 768, 1536, 1664, 1672


def static_rows():
    return [NAT_LOAD + i * 128 for i in range(3)] + [NAT_INV + i * 128 for i in range(6)]


def field_rows():
    return [0, 128, 256, NAT_STIFF]


def pack_y_kernel(
    colour_hbm, disp_hbm, load_hbm, inv_hbm, stiff_hbm,
    lo_ref, hi_ref, order_ref, nat_hbm, nat_ref, colour_s, sems,
):
    moves = [
        (colour_hbm.at[pl.ds(0, 8)], colour_s.at[pl.ds(0, 8)]),
        (colour_hbm.at[pl.ds(16, 8)], colour_s.at[pl.ds(8, 8)]),
        (disp_hbm, nat_ref.at[pl.ds(0, 384)]),
        (stiff_hbm, nat_ref.at[pl.ds(NAT_STIFF, 128)]),
        (load_hbm, nat_ref.at[pl.ds(NAT_LOAD, 384)]),
        (inv_hbm.at[pl.ds(0, 384)], nat_ref.at[pl.ds(NAT_INV, 384)]),
        (inv_hbm.at[pl.ds(512, 256)], nat_ref.at[pl.ds(NAT_INV + 384, 256)]),
        (inv_hbm.at[pl.ds(1024, 128)], nat_ref.at[pl.ds(NAT_INV + 640, 128)]),
    ]
    copies = [pltpu.make_async_copy(a, b, sems.at[i]) for i, (a, b) in enumerate(moves)]
    for copy in copies:
        copy.start()

    def keep(first, count, i):
        part = pl.ds(first, count)
        copy = pltpu.make_async_copy(nat_ref.at[part], nat_hbm.at[part], sems.at[8 + i])
        copy.start()
        return copy

    copies[2].wait()
    copies[3].wait()
    kept = [keep(0, 384, 0), keep(NAT_STIFF, 128, 1)]
    lowm = low(8)
    idx_e = split_idx(8, 0)
    for comp, first in enumerate(field_rows()):
        for py in range(2):
            for out, y1 in ((lo_ref, 0), (hi_ref, 6)):
                a = nat_ref[pl.ds(first + py + 2 * y1, 8, stride=16), :]
                b = nat_ref[pl.ds(first + py + 2 * y1 + 2, 8, stride=16), :]
                if comp == 3:
                    a, b = 0.5 * a, 0.5 * b
                a, b = gather(a, idx_e), gather(b, idx_e)
                row = (comp * 4 + py * 2) * 8
                out[pl.ds(row, 8), :] = jnp.where(lowm, a, swap(b))
                out[pl.ds(row + 8, 8), :] = jnp.where(lowm, swap(a), b)
    copies[0].wait()
    copies[1].wait()
    for cls in range(8):
        px, py, pz = cls >> 2, (cls >> 1) & 1, cls & 1
        order_ref[colour_s[8 * px + py, pz]] = cls
    for k in range(8):
        nat_ref[pl.ds(NAT_ORDER + k, 1), :] = jnp.full((1, 128), order_ref[k].astype(F32))
    kept.append(keep(NAT_ORDER, 8, 3))
    for copy in copies[4:]:
        copy.wait()
    kept.append(keep(NAT_LOAD, 1152, 2))
    sub = lax.broadcasted_iota(jnp.int32, (8, 128), 0)
    second, third, upper = (sub & 3) == 2, (sub & 3) == 3, sub >= 4

    def rows(start, stride):
        return nat_ref[pl.ds(start, 8, stride=stride), :]

    for r in range(2):
        px, py, pz = zip(*[parity(order_ref[4 * r + k]) for k in range(3)])
        cls_row = [px[k] * 16 + py[k] for k in range(3)]
        idx = 2 * (lanes(8) & 63) + jnp.where(second, pz[1], jnp.where(third, pz[2], pz[0]))
        for side, out in ((0, lo_ref), (1, hi_ref)):
            near, far = (0, 1) if side == 0 else (7, 6)
            for a, first in enumerate(static_rows()):
                at = [first + 2 * near + cls_row[k] for k in range(3)]
                at_far = first + 2 * far + cls_row[0]
                nv = jnp.where(upper, rows(at[0] - 64, 32), rows(at[0], 32))
                nv = jnp.where(second, rows(at[1] - 48, 24), jnp.where(third, rows(at[2] - 72, 24), nv))
                fv = jnp.where(upper, rows(at_far - 64, 32), rows(at_far, 32))
                fv = jnp.where(second, rows(at[1] + 16, 8), jnp.where(third, rows(at[2] + 8, 8), fv))
                nv, fv = gather(nv, idx), gather(fv, idx)
                out[pl.ds(NF + (r * 9 + a) * 8, 8), :] = (
                    jnp.where(lowm, nv, fv) if side == 0 else jnp.where(lowm, fv, nv)
                )
    for copy in kept:
        copy.wait()


def convert_kernel(nat_ref, f_ref, s_ref, own0_ref, own1_ref):
    lowm = low(8)
    low4 = low(4)
    idx_e = split_idx(8, 0)
    zero = jnp.zeros((8, 128), F32)
    for comp, first in enumerate(field_rows()):
        for py in range(2):
            ev, od = [], []
            for y1 in range(8):
                v = nat_ref[pl.ds(first + py + 2 * y1, 8, stride=16), :]
                if comp == 3:
                    v = 0.5 * v
                v = gather(v, idx_e)
                ev.append(v)
                od.append(swap(v))
            for l in range(L):
                e0, o0 = (ev[l - 2], od[l - 2]) if l >= 2 else (zero, zero)
                e1, o1 = (ev[l + 4], od[l + 4]) if l <= 3 else (zero, zero)
                row = ((comp * L + l) * 4 + py * 2) * 8
                f_ref[pl.ds(row, 8), :] = jnp.where(lowm, e0, o1)
                f_ref[pl.ds(row + 8, 8), :] = jnp.where(lowm, o0, e1)
    zero4 = jnp.zeros((4, 128), F32)
    for r, own in ((0, own0_ref), (1, own1_ref)):
        for k in range(4):
            px, py, pz = parity(nat_ref[NAT_ORDER + 4 * r + k, 0].astype(jnp.int32))
            cls_row = px * 16 + py
            idx0, idx1 = split_idx(4, pz), split_idx(4, 1 - pz)
            for a, first in enumerate(static_rows()):
                rows = [load_rows(nat_ref, first, cls_row, y1, 4) for y1 in range(8)]
                for l in range(L):
                    v0 = gather(rows[l - 2], idx0) if l >= 2 else zero4
                    v1 = gather(rows[l + 4], idx1) if l <= 3 else zero4
                    v = jnp.where(low4, v0, v1)
                    srow = ((r * 9 + a) * L + l) * 8
                    if k == 0:
                        s_ref[pl.ds(srow, 2), :] = v[0:2]
                        s_ref[pl.ds(srow + 4, 2), :] = v[2:4]
                    else:
                        own[pl.ds((((k - 1) * 9 + a) * L + l) * 4, 4), :] = v
                        if k < 3:
                            s_ref[pl.ds(srow + 1 + k, 1), :] = v[0:1]
                            s_ref[pl.ds(srow + 5 + k, 1), :] = v[3:4]


def add_y(v, l, below, above, lowm):
    if l == 0:
        return jnp.where(lowm, below, v)
    if l == 1:
        return jnp.where(lowm, swap(below), v)
    if l == 4:
        return jnp.where(lowm, v, swap(above))
    if l == 5:
        return jnp.where(lowm, v, above)
    return v


def put_pair(xl_ref, xr_ref, row, v, w):
    sub = lax.broadcasted_iota(jnp.int32, (8, 128), 0) < 4
    xl_ref[pl.ds(row, 8), :] = jnp.where(sub, v, pltpu.roll(w, 4, 0))
    xr_ref[pl.ds(row, 8), :] = jnp.where(sub, pltpu.roll(v, 4, 0), w)


def by_side(one, two, run):
    even = lax.axis_index("gx") % 2 == 0

    @pl.when(even)
    def _():
        run(two, one)

    @pl.when(jnp.logical_not(even))
    def _():
        run(one, two)


def y_masks():
    gy = lax.axis_index("gy")
    return (
        jnp.where(gy > 0, 1.0, 0.0).astype(F32),
        jnp.where(gy < lax.axis_size("gy") - 1, 1.0, 0.0).astype(F32),
    )


def x_masks():
    gx = lax.axis_index("gx")
    return (
        jnp.where(gx > 0, 1.0, 0.0).astype(F32),
        jnp.where(gx < lax.axis_size("gx") - 1, 1.0, 0.0).astype(F32),
    )


def pack_x_fields(comps, f_ref, below_ref, above_ref, xl_ref, xr_ref):
    lowm = low(8)
    m_below, m_above = y_masks()
    for comp in range(comps):
        for half in range(2):
            below = [below_ref[pl.ds((comp * 4 + 2 * half + i) * 8, 8), :] * m_below for i in range(2)]
            above = [above_ref[pl.ds((comp * 4 + 2 * half + i) * 8, 8), :] * m_above for i in range(2)]
            for l in range(L):
                row = (comp * L + l) * 4 + 2 * half
                v = [add_y(f_ref[pl.ds((row + i) * 8, 8), :], l, below[i], above[i], lowm) for i in range(2)]
                put_pair(xl_ref, xr_ref, row * 4, v[0], v[1])


def pack_x_kernel(f_ref, s_ref, above_ref, below_ref, one_ref, two_ref, one_late_ref, two_late_ref):
    pack = functools.partial(pack_x, f_ref, s_ref, below_ref, above_ref)
    by_side((one_ref, one_late_ref), (two_ref, two_late_ref), pack)


def pack_x(f_ref, s_ref, below_ref, above_ref, left, right):
    xl_ref, xr_ref = left[0], right[0]
    pack_x_fields(4, f_ref, below_ref, above_ref, xl_ref, xr_ref)
    lowm = low(8)
    m_below, m_above = y_masks()
    for ra in range(18):
        below = below_ref[pl.ds(NF + ra * 8, 8), :] * m_below
        above = above_ref[pl.ds(NF + ra * 8, 8), :] * m_above
        for l in range(0, L, 2):
            row = ra * L + l
            v = [add_y(s_ref[pl.ds((row + i) * 8, 8), :], l + i, below, above, lowm) for i in range(2)]
            if ra < 9:
                put_pair(xl_ref, xr_ref, XF + row * 4, v[0], v[1])
            else:
                put_pair(left[1], right[1], row * 4 - XS, v[0], v[1])


def pack_x2_kernel(f_ref, above_ref, below_ref, one_ref, two_ref):
    by_side(one_ref, two_ref, functools.partial(pack_x_fields, 3, f_ref, below_ref, above_ref))


def v_row(cls, shifted, comp, ext):
    return PAD + (((cls * 2 + shifted) * 4 + comp) * 8 + ext) * 8


def fill_class(v_ref, cls, pz, comp, v):
    low_edge = pz == 1
    if isinstance(pz, int):
        shift, edge = (1, 0) if low_edge else (127, 63)
        shift_swap = (shift + 64) % 128
    else:
        shift, edge = jnp.where(low_edge, 1, 127), jnp.where(low_edge, 0, 63)
        shift_swap = jnp.where(low_edge, 65, 63)
    keep = (lanes(8) & 63) != edge
    base = v_row(cls, 0, comp, 0)
    moved = v_row(cls, 1, comp, 0)
    for l in (0, L - 1):
        ext = 56 if l == 0 else 0
        v_ref[pl.ds(base + ext, 8), :] = swap(v[l])
        v_ref[pl.ds(moved + ext, 8), :] = jnp.where(keep, pltpu.roll(v[l], shift_swap, 1), 0.0)
    for l in range(L):
        v_ref[pl.ds(moved + (l + 1) * 8, 8), :] = jnp.where(keep, pltpu.roll(v[l], shift, 1), 0.0)


def fill_all(comps, v_ref):
    for comp in range(comps):
        for cls in range(8):
            base = v_row(cls, 0, comp, 1)
            fill_class(v_ref, cls, cls & 1, comp, [v_ref[pl.ds(base + l * 8, 8), :] for l in range(L)])


def place_own(comps, v_ref, e_ref, xl_ref, xr_ref):
    zero = jnp.zeros((8, 128), F32)
    sub = lax.broadcasted_iota(jnp.int32, (8, 128), 0) < 4
    for comp in range(comps):
        for l in range(L):
            for p in (0, 2):
                row = ((comp * L + l) * 4 + p) * 4
                a, b = xl_ref[pl.ds(row, 8), :], xr_ref[pl.ds(row, 8), :]
                at = (l * 4 + p) * 16
                e_ref[pl.ds(at + 4, 8), :] = jnp.where(sub, a, pltpu.roll(b, 4, 0))
                e_ref[pl.ds(at + 20, 8), :] = jnp.where(sub, pltpu.roll(a, 4, 0), b)
        for l in range(L):
            for p in range(4):
                for px in range(2):
                    v_ref[pl.ds(v_row(px * 4 + p, 0, comp, l + 1), 8), :] = e_ref[
                        pl.ds((l * 4 + p) * 16 + px, 8, stride=2), :
                    ]


def place_ghosts(comps, v_ref, rl_ref, rr_ref):
    m_left, m_right = x_masks()
    for comp in range(comps):
        for p in range(4):
            for px in range(2):
                base = v_row(px * 4 + p, 0, comp, 1)
                for i in range(2):
                    row = (comp * L * 4 + p) * 4 + px + 2 * i
                    v_ref[pl.ds(base + i, L, stride=8), :] = rl_ref[pl.ds(row, L, stride=16), :] * m_left
                    v_ref[pl.ds(base + 6 + i, L, stride=8), :] = rr_ref[pl.ds(row, L, stride=16), :] * m_right


def place_own_statics(r, base, st_ref, xl_ref, xr_ref, own_ref, below_ref, above_ref):
    m_below, m_above = y_masks()
    lowm = low(1)
    zero = jnp.zeros((8, 128), F32)
    for a in range(9):
        below = below_ref[pl.ds(NF + (r * 9 + a) * 8, 8), :] * m_below
        above = above_ref[pl.ds(NF + (r * 9 + a) * 8, 8), :] * m_above
        for l in range(L):
            srow = base + (a * L + l) * 4
            own_l, own_r = xl_ref[pl.ds(srow, 4), :], xr_ref[pl.ds(srow, 4), :]
            at = (a * L + l) * 8
            st_ref[pl.ds(at, 8), :] = zero
            st_ref[pl.ds(at + 2, 2), :] = own_l[0:2]
            st_ref[pl.ds(at + 4, 2), :] = own_r[0:2]
            for k in (1, 2, 3):
                at = ((k * 9 + a) * L + l) * 8
                st_ref[pl.ds(at, 8), :] = zero
                st_ref[pl.ds(at + 2, 4), :] = own_ref[pl.ds((((k - 1) * 9 + a) * L + l) * 4, 4), :]
                if k < 3:
                    st_ref[pl.ds(at + 2, 1), :] = own_l[1 + k : 2 + k]
                    st_ref[pl.ds(at + 5, 1), :] = own_r[1 + k : 2 + k]
                    for q in range(2):
                        at_q = at + 3 + q
                        if l == 1:
                            st_ref[pl.ds(at_q, 1), :] = jnp.where(
                                lowm, below[1 + k + 4 * q : 2 + k + 4 * q], st_ref[pl.ds(at_q, 1), :]
                            )
                        if l == 4:
                            st_ref[pl.ds(at_q, 1), :] = jnp.where(
                                lowm, st_ref[pl.ds(at_q, 1), :], above[1 + k + 4 * q : 2 + k + 4 * q]
                            )


def place_ghost_statics(base_row, st_ref, rl_ref, rr_ref):
    m_left, m_right = x_masks()
    for a in range(9):
        for row, k, at_l, at_r in ((0, 0, 0, 6), (1, 0, 1, 7), (2, 1, 1, 6), (3, 2, 1, 6)):
            src = pl.ds(base_row + a * L * 4 + row, L, stride=4)
            base = (k * 9 + a) * L * 8
            st_ref[pl.ds(base + at_l, L, stride=8), :] = rl_ref[src, :] * m_left
            st_ref[pl.ds(base + at_r, L, stride=8), :] = rr_ref[src, :] * m_right


def relax(cls, k, v_ref, st_ref, stencil_ref):
    px, py, pz = parity(cls)
    by_x = {0: 0, -1: px - 1, 1: px}
    by_y = {0: 0, -1: (py - 1) * 8, 1: py * 8}
    by_z = {0: 0, -1: 1 - pz, 1: pz}
    centre = [v_ref[pl.ds(v_row(cls, 0, 3, l + 1), 8), :] for l in range(L)]
    acc = [[None] * L for _ in range(3)]
    fresh = [[None] * L for _ in range(3)]
    for number, (a, b, c) in enumerate(offsets):
        for orient in (1, -1):
            da, db, dc = orient * a, orient * b, orient * c
            source = cls ^ (4 * abs(a) + 2 * abs(b) + abs(c))
            base = v_row(source, by_z[dc], 0, 1) + by_y[db] + by_x[da]
            block = [
                [stencil_ref[number * 9 + (i * 3 + j if orient == 1 else j * 3 + i)] for j in range(3)]
                for i in range(3)
            ]
            for l in range(L):
                weight = centre[l] + v_ref[pl.ds(base + 3 * 64 + l * 8, 8), :]
                wu = [weight * v_ref[pl.ds(base + j * 64 + l * 8, 8), :] for j in range(3)]
                for i in range(3):
                    term = block[i][0] * wu[0] + block[i][1] * wu[1] + block[i][2] * wu[2]
                    acc[i][l] = term if acc[i][l] is None else acc[i][l] + term
    for l in range(L):
        s = [st_ref[pl.ds(((k * 9 + a) * L + l) * 8, 8), :] for a in range(9)]
        rest = [s[i] - acc[i][l] for i in range(3)]
        inv = ((s[3], s[4], s[5]), (s[4], s[6], s[7]), (s[5], s[7], s[8]))
        for i in range(3):
            fresh[i][l] = inv[i][0] * rest[0] + inv[i][1] * rest[1] + inv[i][2] * rest[2]
            v_ref[pl.ds(v_row(cls, 0, i, l + 1), 8), :] = fresh[i][l]

    @pl.when(k < 3)
    def _():
        for i in range(3):
            fill_class(v_ref, cls, pz, i, fresh[i])


def four_colours(r, order_ref, v_ref, st_ref, stencil_ref):
    @pl.loop(0, 4)
    def _(k):
        relax(order_ref[4 * r + k], k, v_ref, st_ref, stencil_ref)


VROWS = 2 * PAD + 8 * 2 * 4 * 64
STROWS = 4 * 9 * L * 8


def prepare_kernel(one_ref, two_ref, own_ref, below_ref, above_ref, v_ref, st_ref, e_ref):
    v_ref[pl.ds(0, PAD), :] = jnp.zeros((PAD, 128), F32)
    v_ref[pl.ds(VROWS - PAD, PAD), :] = jnp.zeros((PAD, 128), F32)

    def place(xl_ref, xr_ref):
        place_own(4, v_ref, e_ref, xl_ref, xr_ref)
        place_own_statics(0, XF, st_ref, xl_ref, xr_ref, own_ref, below_ref, above_ref)

    by_side(one_ref, two_ref, place)


def first_kernel(order_ref, stencil_ref, two_ref, one_ref, _v, _st, v_ref, st_ref, lo_ref, hi_ref):

    def place(rl_ref, rr_ref):
        place_ghosts(4, v_ref, rl_ref, rr_ref)
        place_ghost_statics(XF, st_ref, rl_ref, rr_ref)

    by_side(one_ref, two_ref, place)
    fill_all(4, v_ref)
    four_colours(0, order_ref, v_ref, st_ref, stencil_ref)
    lowm = low(4)
    for comp in range(3):
        for p in range(4):
            for px in range(2):
                at = v_row(px * 4 + p, 0, comp, 3) + 2
                v2, v3 = v_ref[pl.ds(at, 4), :], v_ref[pl.ds(at + 8, 4), :]
                to = pl.ds((comp * 4 + p) * 8 + px, 4, stride=2)
                lo_ref[to, :] = jnp.where(lowm, v2, swap(v3))
                hi_ref[to, :] = jnp.where(lowm, swap(v2), v3)


def between_kernel(v_ref, r1_ref, x1_ref, x2_ref, r2_ref, own_ref, below_ref, above_ref, f_ref, st_ref):
    for comp in range(3):
        for l in range(L):
            for p in range(4):
                for px in range(2):
                    f_ref[pl.ds(((comp * L + l) * 4 + p) * 8 + px, 4, stride=2), :] = v_ref[
                        pl.ds(v_row(px * 4 + p, 0, comp, l + 1) + 2, 4), :
                    ]

    def place(left, right):
        place_own_statics(1, 0, st_ref, left[0], right[0], own_ref, below_ref, above_ref)
        place_ghost_statics(0, st_ref, left[1], right[1])

    by_side((x1_ref, r1_ref), (x2_ref, r2_ref), place)


def prepare2_kernel(one_ref, two_ref, _v, v_ref, e_ref):
    by_side(one_ref, two_ref, functools.partial(place_own, 3, v_ref, e_ref))


def second_kernel(order_ref, stencil_ref, two_ref, one_ref, st_ref, _v, v_ref, out_ref):
    by_side(one_ref, two_ref, functools.partial(place_ghosts, 3, v_ref))
    fill_all(3, v_ref)
    four_colours(1, order_ref, v_ref, st_ref, stencil_ref)
    lowm = low(4)
    lane = lanes(4)
    merge = lax.shift_right_logical(lane, 1) + 64 * (lane & 1)
    for comp in range(3):
        for px in range(2):
            for py in range(2):
                cls = px * 4 + py * 2
                for l in range(L):
                    ev = v_ref[pl.ds(v_row(cls, 0, comp, l + 1) + 2, 4), :]
                    od = v_ref[pl.ds(v_row(cls + 1, 0, comp, l + 1) + 2, 4), :]
                    first = comp * 128 + px * 16 + py
                    if l >= 2:
                        out_ref[pl.ds(first + 2 * (l - 2), 4, stride=32), :] = gather(
                            jnp.where(lowm, ev, swap(od)), merge
                        )
                    if l <= 3:
                        out_ref[pl.ds(first + 2 * (l + 4), 4, stride=32), :] = gather(
                            jnp.where(lowm, swap(ev), od), merge
                        )


SMEM = pl.BlockSpec(memory_space=pltpu.SMEM)
VMEM = pl.BlockSpec(memory_space=pltpu.VMEM)


HBM = pl.BlockSpec(memory_space=pltpu.HBM)


def call(kernel, specs, outs, scratch, cost, aliases={}, vmem=24, extra_outs=(), extra_out_specs=(), extra_scratch=()):
    return pl.pallas_call(
        kernel,
        in_specs=specs,
        out_shape=tuple(jax.ShapeDtypeStruct((n, 128), F32) for n in outs) + tuple(extra_outs),
        out_specs=tuple(VMEM for _ in outs) + tuple(extra_out_specs),
        scratch_shapes=[pltpu.VMEM((n, 128), F32) for n in scratch] + list(extra_scratch),
        input_output_aliases=aliases,
        compiler_params=pltpu.CompilerParams(vmem_limit_bytes=vmem * 1024 * 1024),
        cost_estimate=pl.CostEstimate(flops=cost, bytes_accessed=cost, transcendentals=0),
    )


def ring(value, axis, step):
    count = lax.axis_size(axis)
    return lax.ppermute(value, axis, [(i, (i + step) % count) for i in range(count)])


def swaps(one, two):
    n = lax.axis_size("gx")
    first = [(i, i ^ 1) for i in range(n)]
    second = [(i, (i + 1 if i % 2 else i - 1) % n) for i in range(n)]
    far = lax.ppermute(two, "gx", second)
    return lax.ppermute(one, "gx", first), far


def per_device(displacement, load_vector, diag_inverse, stiffness, stencil, colour):
    disp = displacement.reshape(3 * 128, 128)
    load = load_vector.reshape(3 * 128, 128)
    inv = diag_inverse.reshape(9 * 128, 128)
    stiff = stiffness.reshape(128, 128)
    colours = colour.reshape(128, 128)
    coefs = stencil.reshape(117)

    lo, hi, order, nat = call(
        pack_y_kernel,
        [HBM] * 5,
        (NF + NS, NF + NS),
        (NAT_ROWS,),
        1 << 20,
        vmem=56,
        extra_outs=[jax.ShapeDtypeStruct((8,), jnp.int32), jax.ShapeDtypeStruct((NAT_ROWS, 128), F32)],
        extra_out_specs=[SMEM, HBM],
        extra_scratch=[pltpu.SMEM((16, 128), jnp.int32), pltpu.SemaphoreType.DMA((12,))],
    )(colours, disp, load, inv, stiff)
    above = ring(lo, "gy", -1)
    below = ring(hi, "gy", 1)
    f, s, own0, own1 = call(convert_kernel, [VMEM], (768, 864, 648, 648), (), 1 << 22)(nat)
    x1, x2, late1, late2 = call(pack_x_kernel, [VMEM] * 4, (XF + XS, XF + XS, XS, XS), (), 1 << 20)(f, s, above, below)
    r1, r2 = swaps(x1, x2)
    got1, got2 = swaps(late1, late2)
    v, st = call(prepare_kernel, [VMEM] * 5, (VROWS, STROWS), (384,), 1 << 22)(x1, x2, own0, below, above)
    v, _, lo2, hi2 = call(
        first_kernel, [SMEM] * 2 + [VMEM] * 4, (VROWS, STROWS, 96, 96), (), 1 << 24, aliases={4: 0, 5: 1}
    )(order, coefs, r2, r1, v, st)
    above2 = ring(lo2, "gy", -1)
    below2 = ring(hi2, "gy", 1)
    f2, st = call(between_kernel, [VMEM] * 8, (576, STROWS), (), 1 << 22)(v, got1, late1, late2, got2, own1, below, above)
    x1, x2 = call(pack_x2_kernel, [VMEM] * 3, (288, 288), (), 1 << 20)(f2, above2, below2)
    r1, r2 = swaps(x1, x2)
    (v,) = call(prepare2_kernel, [VMEM] * 3, (VROWS,), (384,), 1 << 22, aliases={2: 0})(x1, x2, v)
    v, out = call(second_kernel, [SMEM] * 2 + [VMEM] * 4, (VROWS, 384), (), 1 << 24, aliases={5: 0})(
        order, coefs, r2, r1, st, v
    )
    return out.reshape(3, XD, YD, ZD)


def solution(mesh):
    return jax.shard_map(
        per_device,
        mesh=mesh,
        in_specs=(
            P(None, "gx", "gy", None),
            P(None, "gx", "gy", None),
            P(None, None, "gx", "gy", None),
            P("gx", "gy", None),
            P(),
            P("gx", "gy", None),
        ),
        out_specs=P(None, "gx", "gy", None),
        check_vma=False,
    )
```
